32 devices in a mesh: dp: 4 (over y, core), ctx: 8 (over z, x).
Axes of the slice: x: 2, y: 2, z: 4, core: 2. Of those that a mesh axis runs over, the one named last changes fastest.
Arguments:
- context_query_rows: bfloat16 [4096, 4096], P(('dp', 'ctx')), parts along dimension 0, may hold values from -16 to 16
- context_key_rows: bfloat16 [4096, 512], P(('dp', 'ctx')), parts along dimension 0, may hold values from -6 to 6
- context_value_rows: bfloat16 [4096, 512], P(('dp', 'ctx')), parts along dimension 0, may hold values from -6 to 6
- question_query_rows: bfloat16 [1024, 4096], P(('dp', 'ctx')), parts along dimension 0, may hold values from -16 to 16
- token_mask: int32 [4096], P(('dp', 'ctx')), parts along dimension 0, may hold values 0 or 1
- live_blocks: int32 [4], P('dp'), parts along dimension 0, may hold values from 4 to 8
Outputs:
- context_output: bfloat16 [4096, 4096], P(('dp', 'ctx')), parts along dimension 0
- query_output: bfloat16 [1024, 4096], P(('dp', 'ctx')), parts along dimension 0
The draws below stay inside these ranges and needn't reach their ends.
There are 4 independent parts, one for each index of `dp`. The reference program is written for one: setup_inputs(seed, part) draws one part's arguments, and reference() takes and returns one part's arrays. A program takes and returns all parts, laid end to end along the dimension named above; each array names one. Nothing has to cross between parts.
All inputs are finite; a program needn't handle non-finite values. No bound on the sum of `token_mask` on one device may be relied on, other than what follows from the above.
Results may differ from the reference program's by a relative error of at most 0.0026.
Values may be sent and summed in bfloat16 or wider, within the bound.
No kernel may reach another device: no remote copies, remote signals or barrier semaphores. Data moves between devices by JAX's collectives and lax.ppermute only.
A program may use at most 64 MiB of HBM per device.

```python
import jax
import jax.numpy as jnp
from jax import lax

QUERY_HEADS = 32
KEY_VALUE_HEADS = 4
HEAD_SIZE = 128
BLOCK_TOKENS = 128
QUERY_TOKENS = 256
CONTEXT_TOKENS = 1024
N_CTX = 8


def draw_context_key_rows(key, part):
    key = jax.random.fold_in(key, 11)
    array_shape = (BLOCK_TOKENS * N_CTX, KEY_VALUE_HEADS * HEAD_SIZE)
    base = jnp.clip(jax.random.normal(key, array_shape, jnp.float32), -6.0, 6.0)
    return base.astype(jnp.bfloat16)


def draw_context_query_rows(key, part):
    key = jax.random.fold_in(key, 23)
    array_shape = (BLOCK_TOKENS * N_CTX, QUERY_HEADS * HEAD_SIZE)
    base = jnp.clip(3.0 * jax.random.normal(key, array_shape, jnp.float32), -16.0, 16.0)
    return base.astype(jnp.bfloat16)


def draw_question_query_rows(key, part):
    key = jax.random.fold_in(key, 37)
    array_shape = (QUERY_TOKENS, QUERY_HEADS * HEAD_SIZE)
    base = jnp.clip(3.0 * jax.random.normal(key, array_shape, jnp.float32), -16.0, 16.0)
    return base.astype(jnp.bfloat16)


def plant(values, stream_key, least, top_value):
    shape = values.shape
    place = [jax.random.randint(jax.random.fold_in(stream_key, axis), (), 0, shape[axis]) for axis in range(len(shape))]
    values = values.at[tuple(place)].set(least)
    longest = shape.index(max(shape))
    place[longest] = (place[longest] + 1) % shape[longest]
    return values.at[tuple(place)].set(top_value)


def block_scale(own_key, shape, shards, smallest, high):
    def one(position, parts):
        heights = jax.random.uniform(jax.random.fold_in(jax.random.fold_in(own_key, 6), position), (parts,), jnp.float32, smallest / len(shards), high / len(shards))
        return jnp.repeat(jnp.exp(heights), shape[position] // parts).reshape((-1,) + (1,) * (len(shape) - position - 1))

    loudness = one(*shards[0])
    for cut in shards[1:]:
        loudness = loudness * one(*cut)
    return loudness


def gaussian(stream_key, extent, deviation, limit, shards=(), kind=jnp.bfloat16):
    values = jax.random.normal(stream_key, extent, jnp.float32) * deviation
    if len(shards) > 0:
        values = block_scale(stream_key, extent, shards, -0.22, 0.18) * values
    return jnp.clip(values, min=-limit, max=limit).astype(kind)


def setup_inputs(seed: int = 0, part: int = 0) -> dict:
    streams_of = jax.random.split(jax.random.key(seed), 7)
    part_keys = jax.random.split(jax.random.fold_in(streams_of[6], part), 7)
    context_query_rows = draw_context_query_rows(jax.random.fold_in(jax.random.fold_in(streams_of[6], part), 71), part)
    context_key_rows = draw_context_key_rows(jax.random.fold_in(jax.random.fold_in(streams_of[6], part), 71), part)
    context_value_rows = gaussian(part_keys[2], (CONTEXT_TOKENS, KEY_VALUE_HEADS * HEAD_SIZE), 1.0, 6.0, ((0, 8),))
    question_query_rows = draw_question_query_rows(jax.random.fold_in(jax.random.fold_in(streams_of[6], part), 71), part)
    token_mask = plant((jax.random.randint(part_keys[4], (CONTEXT_TOKENS,), 0, 8) < 7).astype(jnp.int32), jax.random.fold_in(part_keys[4], 1), 0, 1)
    live_blocks = jax.random.randint(part_keys[5], (1,), N_CTX // 2, N_CTX + 1).astype(jnp.int32)
    return {"context_query_rows": context_query_rows, "context_key_rows": context_key_rows, "context_value_rows": context_value_rows, "question_query_rows": question_query_rows, "token_mask": token_mask, "live_blocks": live_blocks}


def reference(context_query_rows, context_key_rows, context_value_rows, question_query_rows, token_mask, live_blocks):
    inv_root = HEAD_SIZE ** -0.5
    heads_per_group = QUERY_HEADS // KEY_VALUE_HEADS
    positions = jnp.arange(BLOCK_TOKENS * N_CTX, dtype=jnp.int32)
    key_valid = ((token_mask != 0) | (positions == 0)) & (positions // BLOCK_TOKENS < live_blocks[0])
    leading_block_keys = context_key_rows[:BLOCK_TOKENS].astype(jnp.float32).reshape(BLOCK_TOKENS, KEY_VALUE_HEADS, HEAD_SIZE)
    leading_block_values = context_value_rows[:BLOCK_TOKENS].astype(jnp.float32).reshape(BLOCK_TOKENS, KEY_VALUE_HEADS, HEAD_SIZE)
    anchor_valid = key_valid[:BLOCK_TOKENS]
    local_rows = jnp.arange(BLOCK_TOKENS, dtype=jnp.int32)
    causal = local_rows[None, :] <= local_rows[:, None]
    diagonal = local_rows[None, :] == local_rows[:, None]

    def context_block(block_index):
        start_position = (block_index * BLOCK_TOKENS).astype(jnp.int32)
        query_vectors = lax.dynamic_slice_in_dim(context_query_rows, start_position, BLOCK_TOKENS, 0).astype(jnp.float32).reshape(BLOCK_TOKENS, KEY_VALUE_HEADS, heads_per_group, HEAD_SIZE)
        local_block_keys = lax.dynamic_slice_in_dim(context_key_rows, start_position, BLOCK_TOKENS, 0).astype(jnp.float32).reshape(BLOCK_TOKENS, KEY_VALUE_HEADS, HEAD_SIZE)
        local_block_values = lax.dynamic_slice_in_dim(context_value_rows, start_position, BLOCK_TOKENS, 0).astype(jnp.float32).reshape(BLOCK_TOKENS, KEY_VALUE_HEADS, HEAD_SIZE)
        own_valid = lax.dynamic_slice_in_dim(key_valid, start_position, BLOCK_TOKENS, 0)
        all_keys = jnp.concatenate([leading_block_keys, local_block_keys], 0)
        all_vals = jnp.concatenate([leading_block_values, local_block_values], 0)
        see_anchor = jnp.broadcast_to(anchor_valid[None, :] & (block_index > 0), (BLOCK_TOKENS, BLOCK_TOKENS))
        see_own = (own_valid[None, :] & causal) | diagonal
        visible = jnp.concatenate([see_anchor, see_own], 1)
        scores = jnp.einsum("qhgd,khd->hgqk", query_vectors, all_keys) * inv_root
        scores = jnp.where(visible, scores, -1e30)
        row_top = jnp.max(scores, axis=-1, keepdims=True)
        weights = jnp.where(visible, jnp.exp(scores - row_top), 0.0)
        row_total = jnp.sum(weights, axis=-1)
        rounded = lax.optimization_barrier(weights.astype(jnp.bfloat16)).astype(jnp.float32)
        mixed = jnp.einsum("hgqk,khd->qhgd", rounded, all_vals)
        mixed = mixed / jnp.transpose(row_total, (2, 0, 1))[:, :, :, None]
        is_live = (block_index < live_blocks[0]).astype(jnp.float32)
        return (mixed.reshape(BLOCK_TOKENS, QUERY_HEADS * HEAD_SIZE) * is_live).astype(jnp.bfloat16)

    context_output = lax.map(context_block, jnp.arange(N_CTX, dtype=jnp.int32)).reshape(BLOCK_TOKENS * N_CTX, QUERY_HEADS * HEAD_SIZE)

    gathered_query_vectors = question_query_rows.astype(jnp.float32).reshape(QUERY_TOKENS, KEY_VALUE_HEADS, heads_per_group, HEAD_SIZE)

    def query_block(block_index):
        start_position = (block_index * BLOCK_TOKENS).astype(jnp.int32)
        local_block_keys = lax.dynamic_slice_in_dim(context_key_rows, start_position, BLOCK_TOKENS, 0).astype(jnp.float32).reshape(BLOCK_TOKENS, KEY_VALUE_HEADS, HEAD_SIZE)
        local_block_values = lax.dynamic_slice_in_dim(context_value_rows, start_position, BLOCK_TOKENS, 0).astype(jnp.float32).reshape(BLOCK_TOKENS, KEY_VALUE_HEADS, HEAD_SIZE)
        own_valid = lax.dynamic_slice_in_dim(key_valid, start_position, BLOCK_TOKENS, 0)
        scores = jnp.einsum("qhgd,khd->hgqk", gathered_query_vectors, local_block_keys) * inv_root
        scores = jnp.where(own_valid, scores, -1e30)
        row_top = jnp.max(scores, axis=-1)
        weights = jnp.where(own_valid, jnp.exp(scores - row_top[..., None]), 0.0)
        row_total = jnp.sum(weights, axis=-1)
        rounded = lax.optimization_barrier(weights.astype(jnp.bfloat16)).astype(jnp.float32)
        block_part = jnp.einsum("hgqk,khd->hgqd", rounded, local_block_values)
        return row_top, row_total, block_part

    block_tops, block_totals, block_parts = lax.map(query_block, jnp.arange(N_CTX, dtype=jnp.int32))
    global_top = jnp.max(block_tops, axis=0)
    factor = jnp.exp(block_tops - global_top[None])
    numerator = jnp.sum(factor[..., None] * block_parts, axis=0)
    denominator = jnp.sum(factor * block_totals, axis=0)
    result = numerator / denominator[..., None]
    query_output = jnp.transpose(result, (2, 0, 1, 3)).reshape(QUERY_TOKENS, QUERY_HEADS * HEAD_SIZE).astype(jnp.bfloat16)
    return context_output, query_output
```

```python
import functools

import jax
import jax.numpy as jnp
from jax import lax
from jax.experimental import pallas as pl
from jax.experimental.pallas import tpu as pltpu
from jax.sharding import PartitionSpec as P

HEAD = 128
FLAG_ROWS = 16
HIDDEN = -1e30
NT = (((1,), (1,)), ((), ()))


def whole():
    return pl.BlockSpec(memory_space=pltpu.VMEM)


def scalar():
    return pl.BlockSpec(memory_space=pltpu.SMEM)


def pack_kernel(live_ref, mask_ref, k_ref, v_ref, o_ref):
    rows, width = k_ref.shape
    groups = width // HEAD
    block = lax.axis_index("ctx")
    for g in range(groups):
        o_ref[g * rows : (g + 1) * rows, :] = k_ref[:, g * HEAD : (g + 1) * HEAD]
        o_ref[(groups + g) * rows : (groups + g + 1) * rows, :] = v_ref[:, g * HEAD : (g + 1) * HEAD]
    token = lax.broadcasted_iota(jnp.int32, (1, rows), 1)
    valid = ((mask_ref[...] != 0) | ((block == 0) & (token == 0))) & (block < live_ref[0])
    flags = jnp.where(valid, 1.0, 0.0).astype(jnp.bfloat16)
    o_ref[2 * groups * rows :, :] = jnp.broadcast_to(flags, (FLAG_ROWS, rows))


def pack(live_blocks, token_mask, k, v):
    rows, width = k.shape
    return pl.pallas_call(
        pack_kernel,
        out_shape=jax.ShapeDtypeStruct((2 * rows * width // HEAD + FLAG_ROWS, HEAD), jnp.bfloat16),
        in_specs=[scalar(), whole(), whole(), whole()],
        out_specs=whole(),
        name="pack",
    )(live_blocks, token_mask.reshape(1, rows), k, v)


def context_kernel(pieces, rows, groups, live_ref, q_ref, *refs):
    piece_refs, o_ref, anchor = refs[:pieces], refs[pieces], refs[pieces + 1]
    g = pl.program_id(0)
    block = lax.axis_index("ctx")

    @pl.when(g == 0)
    def _():
        for d in range(pieces):

            @pl.when(block == d)
            def _():
                anchor[...] = piece_refs[d][...]

    own = piece_refs[0]
    k_at = pl.ds(pl.multiple_of(g * rows, rows), rows)
    v_at = pl.ds(pl.multiple_of((groups + g) * rows, rows), rows)
    keys = jnp.concatenate([anchor[k_at, :], own[k_at, :]], 0)
    values = jnp.concatenate([anchor[v_at, :], own[v_at, :]], 0)
    flag_at = 2 * groups * rows
    i = lax.broadcasted_iota(jnp.int32, (rows, rows), 0)
    j = lax.broadcasted_iota(jnp.int32, (rows, rows), 1)
    anchor_flag = anchor[flag_at : flag_at + FLAG_ROWS, :].astype(jnp.float32)[:1]
    own_flag = own[flag_at : flag_at + FLAG_ROWS, :].astype(jnp.float32)[:1]
    see_anchor = jnp.broadcast_to(anchor_flag, (rows, rows)) * jnp.where(block > 0, 1.0, 0.0)
    see_own = jnp.where(j < i, jnp.broadcast_to(own_flag, (rows, rows)), jnp.where(i == j, 1.0, 0.0))
    visible = jnp.concatenate([see_anchor, see_own], 1) > 0.5
    alive = jnp.where(block < live_ref[0], 1.0, 0.0)
    for h in range(q_ref.shape[1] // HEAD):
        q = q_ref[:, h * HEAD : (h + 1) * HEAD]
        s = lax.dot_general(q, keys, NT, preferred_element_type=jnp.float32) * HEAD**-0.5
        s = jnp.where(visible, s, HIDDEN)
        m = jnp.max(s, axis=1, keepdims=True)
        p = jnp.where(visible, jnp.exp(s - m), 0.0)
        l = jnp.sum(p, axis=1, keepdims=True)
        a = jnp.dot(p.astype(jnp.bfloat16), values, preferred_element_type=jnp.float32)
        o_ref[:, h * HEAD : (h + 1) * HEAD] = (a * (alive / l)).astype(o_ref.dtype)


def context(live_blocks, q, pieces, groups):
    rows, width = q.shape
    share = width // groups
    return pl.pallas_call(
        functools.partial(context_kernel, len(pieces), rows, groups),
        out_shape=jax.ShapeDtypeStruct(q.shape, q.dtype),
        grid=(groups,),
        in_specs=[scalar(), pl.BlockSpec((rows, share), lambda g: (0, g))] + [whole()] * len(pieces),
        out_specs=pl.BlockSpec((rows, share), lambda g: (0, g)),
        scratch_shapes=[pltpu.VMEM(pieces[0].shape, pieces[0].dtype)],
        name="context",
    )(live_blocks, q, *pieces)


def query_kernel(pieces, rows, groups, q_ref, *refs):
    piece_refs, o_ref = refs[:pieces], refs[pieces]
    n_q, width = q_ref.shape
    heads = width // HEAD // groups
    flag_at = 2 * groups * rows
    for g in range(groups):
        first = g * heads
        q = jnp.concatenate(
            [q_ref[:, (first + h) * HEAD : (first + h + 1) * HEAD].astype(jnp.float32) for h in range(heads)], 0
        ).astype(jnp.bfloat16)
        tops, totals, parts = [], [], []
        for ref in piece_refs:
            flag = ref[flag_at : flag_at + FLAG_ROWS, :].astype(jnp.float32)[:1]
            valid = jnp.broadcast_to(flag, (q.shape[0], rows)) > 0.5
            s = lax.dot_general(q, ref[g * rows : (g + 1) * rows, :], NT, preferred_element_type=jnp.float32)
            s = jnp.where(valid, s * HEAD**-0.5, HIDDEN)
            m = jnp.max(s, axis=1, keepdims=True)
            p = jnp.where(valid, jnp.exp(s - m), 0.0)
            tops.append(m)
            totals.append(jnp.sum(p, axis=1, keepdims=True))
            v = ref[(groups + g) * rows : (groups + g + 1) * rows, :]
            parts.append(jnp.dot(p.astype(jnp.bfloat16), v, preferred_element_type=jnp.float32))
        top = functools.reduce(jnp.maximum, tops)
        factors = [jnp.exp(m - top) for m in tops]
        total = sum(f * l for f, l in zip(factors, totals))
        part = sum(f * a for f, a in zip(factors, parts)) / total
        for h in range(heads):
            o_ref[:, (first + h) * HEAD : (first + h + 1) * HEAD] = part[h * n_q : (h + 1) * n_q].astype(o_ref.dtype)


def query(q, pieces, rows, groups):
    return pl.pallas_call(
        functools.partial(query_kernel, len(pieces), rows, groups),
        out_shape=jax.ShapeDtypeStruct(q.shape, q.dtype),
        in_specs=[whole()] * (1 + len(pieces)),
        out_specs=whole(),
        name="query",
    )(q, *pieces)


def gather(own, n):
    def swap(value, d):
        return lax.ppermute(value, "ctx", [(i, i ^ d) for i in range(n)])

    pieces = {0: own}
    for d in range(2, n, 2):
        pieces[d] = swap(own, d)
    pieces[1] = swap(own, 1)
    for d in range(2, n, 2):
        pieces[d + 1] = swap(pieces[d], 1)
    return [pieces[d] for d in range(n)]


def local(context_q, context_k, context_v, question_q, token_mask, live_blocks):
    n = lax.axis_size("ctx")
    rows, width = context_k.shape
    groups = width // HEAD
    own = pack(live_blocks, token_mask, context_k, context_v)
    pieces = gather(own, n)
    context_output = context(live_blocks, context_q, pieces, groups)
    query_output = query(question_q, pieces, rows, groups)
    return context_output, query_output


def solution(mesh):
    rows = P(("dp", "ctx"), None)
    return jax.shard_map(
        local,
        mesh=mesh,
        in_specs=(rows, rows, rows, rows, P(("dp", "ctx")), P("dp")),
        out_specs=(rows, rows),
        check_vma=False,
    )
```

```python
import functools
import math

import jax
import jax.numpy as jnp
from jax import lax
from jax.experimental import pallas as pl
from jax.experimental.pallas import tpu as pltpu
from jax.sharding import PartitionSpec as P

HEAD = 128
FLAG_ROWS = 16
HIDDEN = -1e30
SCALE = HEAD**-0.5 / math.log(2.0)
NT = (((1,), (1,)), ((), ()))
F32 = jnp.float32
BF16 = jnp.bfloat16
LIMIT = pltpu.CompilerParams(vmem_limit_bytes=24 * 1024 * 1024)


def whole():
    return pl.BlockSpec(memory_space=pltpu.VMEM)


def scalar():
    return pl.BlockSpec(memory_space=pltpu.SMEM)


def anywhere():
    return pl.BlockSpec(memory_space=pl.ANY)


def transposed_flags(ref, groups, rows):
    at = 2 * groups * rows
    flags = ref[at : at + FLAG_ROWS, :].astype(F32)[:1]
    return jnp.transpose(jnp.broadcast_to(flags, (rows, rows)))


def pack_kernel(live_ref, mask_ref, k_ref, v_ref, o_ref):
    rows, width = k_ref.shape
    groups = width // HEAD
    block = lax.axis_index("ctx")
    for g in range(groups):
        o_ref[g * rows : (g + 1) * rows, :] = k_ref[:, g * HEAD : (g + 1) * HEAD]
        o_ref[(groups + g) * rows : (groups + g + 1) * rows, :] = jnp.transpose(v_ref[:, g * HEAD : (g + 1) * HEAD])
    token = lax.broadcasted_iota(jnp.int32, (1, rows), 1)
    valid = ((mask_ref[...] != 0) | ((block == 0) & (token == 0))) & (block < live_ref[0])
    flags = jnp.where(valid, 1.0, 0.0).astype(BF16)
    o_ref[2 * groups * rows :, :] = jnp.broadcast_to(flags, (FLAG_ROWS, rows))


def pack(live_blocks, token_mask, k, v):
    rows, width = k.shape
    return pl.pallas_call(
        pack_kernel,
        out_shape=jax.ShapeDtypeStruct((2 * rows * width // HEAD + FLAG_ROWS, HEAD), BF16),
        in_specs=[scalar(), whole(), whole(), whole()],
        out_specs=whole(),
        compiler_params=LIMIT,
        name="pack",
    )(live_blocks, token_mask.reshape(1, rows), k, v)


def attend(ref, g, groups, rows, q, seen):
    s = lax.dot_general(ref[g * rows : (g + 1) * rows, :], q, NT, preferred_element_type=F32)
    s = jnp.where(seen, s, HIDDEN)
    m = jnp.max(s, axis=0, keepdims=True)
    p = jnp.exp2((s - m) * SCALE)
    l = jnp.sum(p, axis=0, keepdims=True)
    v = ref[(groups + g) * rows : (groups + g + 1) * rows, :]
    return m, l, jnp.dot(v, p.astype(BF16), preferred_element_type=F32)


def merge(one, two):
    top = jnp.maximum(one[0], two[0])
    f, h = jnp.exp2((one[0] - top) * SCALE), jnp.exp2((two[0] - top) * SCALE)
    return top, one[1] * f + two[1] * h, one[2] * f + two[2] * h


def seen_by_all(ref, groups, rows, lanes):
    flags = transposed_flags(ref, groups, rows)
    while flags.shape[1] < lanes:
        flags = jnp.concatenate([flags, flags], 1)
    return flags[:, :lanes] > 0.5


def load_state(acc_ref, stat_ref, g):
    return stat_ref[2 * g : 2 * g + 1, :], stat_ref[2 * g + 1 : 2 * g + 2, :], acc_ref[g * HEAD : (g + 1) * HEAD, :]


def store_state(acc_ref, stat_ref, g, state):
    stat_ref[2 * g : 2 * g + 1, :] = state[0]
    stat_ref[2 * g + 1 : 2 * g + 2, :] = state[1]
    acc_ref[g * HEAD : (g + 1) * HEAD, :] = state[2]


def first_kernel(groups, rows, q_ref, piece, stacked, acc, stat):
    n_q, width = q_ref.shape
    heads = width // HEAD // groups
    lanes = heads * n_q
    seen = seen_by_all(piece, groups, rows, lanes)
    for g in range(groups):
        q = jnp.concatenate(
            [q_ref[:, (g * heads + h) * HEAD : (g * heads + h + 1) * HEAD].astype(F32) for h in range(heads)], 0
        ).astype(BF16)
        stacked[g * lanes : (g + 1) * lanes, :] = q
        store_state(acc, stat, g, attend(piece, g, groups, rows, q, seen))


def state_shapes(groups, lanes):
    return [
        jax.ShapeDtypeStruct((groups * HEAD, lanes), F32),
        jax.ShapeDtypeStruct((2 * groups, lanes), F32),
    ]


def query_first(q, piece, groups, rows):
    n_q, width = q.shape
    lanes = n_q * width // HEAD // groups
    return pl.pallas_call(
        functools.partial(first_kernel, groups, rows),
        out_shape=[jax.ShapeDtypeStruct((groups * lanes, HEAD), BF16)] + state_shapes(groups, lanes),
        in_specs=[whole()] * 2,
        out_specs=[whole()] * 3,
        compiler_params=LIMIT,
        name="query_first",
    )(q, piece)


def more_kernel(groups, rows, count, stacked, acc_in, stat_in, *refs):
    pieces, (acc, stat) = refs[:count], refs[count:]
    lanes = stacked.shape[0] // groups
    seen = [seen_by_all(piece, groups, rows, lanes) for piece in pieces]
    for g in range(groups):
        q = stacked[g * lanes : (g + 1) * lanes, :]
        state = load_state(acc_in, stat_in, g)
        for piece, mask in zip(pieces, seen):
            state = merge(state, attend(piece, g, groups, rows, q, mask))
        store_state(acc, stat, g, state)


def query_more(stacked, acc, stat, pieces, groups, rows):
    return pl.pallas_call(
        functools.partial(more_kernel, groups, rows, len(pieces)),
        out_shape=state_shapes(groups, stacked.shape[0] // groups),
        in_specs=[whole()] * (3 + len(pieces)),
        out_specs=[whole()] * 2,
        input_output_aliases={1: 0, 2: 1},
        compiler_params=LIMIT,
        name="query_more",
    )(stacked, acc, stat, *pieces)


def last_kernel(groups, rows, count, stacked, acc_in, stat_in, *refs):
    pieces, o_ref = refs[:count], refs[count]
    lanes = stacked.shape[0] // groups
    n_q, width = o_ref.shape
    heads = width // HEAD // groups
    seen = [seen_by_all(piece, groups, rows, lanes) for piece in pieces]
    for g in range(groups):
        q = stacked[g * lanes : (g + 1) * lanes, :]
        state = load_state(acc_in, stat_in, g)
        for piece, mask in zip(pieces, seen):
            state = merge(state, attend(piece, g, groups, rows, q, mask))
        out = jnp.transpose(state[2] / state[1])
        for h in range(heads):
            o_ref[:, (g * heads + h) * HEAD : (g * heads + h + 1) * HEAD] = out[h * n_q : (h + 1) * n_q].astype(BF16)


def query_last(stacked, acc, stat, pieces, groups, rows, shape):
    return pl.pallas_call(
        functools.partial(last_kernel, groups, rows, len(pieces)),
        out_shape=shape,
        in_specs=[whole()] * (3 + len(pieces)),
        out_specs=whole(),
        compiler_params=LIMIT,
        name="query_last",
    )(stacked, acc, stat, *pieces)


def context_body(groups, rows, live_ref, q_ref, anchor, own, o_ref, q_buf, o_buf, in_sems, out_sems):
    block = lax.axis_index("ctx")
    share = q_ref.shape[1] // groups
    loads = [
        pltpu.make_async_copy(q_ref.at[:, pl.ds(g * share, share)], q_buf.at[:, pl.ds(g * share, share)], in_sems.at[g])
        for g in range(groups)
    ]
    stores = [
        pltpu.make_async_copy(o_buf.at[:, pl.ds(g * share, share)], o_ref.at[:, pl.ds(g * share, share)], out_sems.at[g])
        for g in range(groups)
    ]
    for load in loads:
        load.start()
    key = lax.broadcasted_iota(jnp.int32, (rows, rows), 0)
    row = lax.broadcasted_iota(jnp.int32, (rows, rows), 1)
    see_anchor = transposed_flags(anchor, groups, rows) * jnp.where(block > 0, 1.0, 0.0)
    see_own = jnp.where(key < row, transposed_flags(own, groups, rows), jnp.where(key == row, 1.0, 0.0))
    visible = jnp.concatenate([see_anchor, see_own], 0) > 0.5
    alive = jnp.where(block < live_ref[0], 1.0, 0.0)
    for g in range(groups):
        k_at = slice(g * rows, (g + 1) * rows)
        v_at = slice((groups + g) * rows, (groups + g + 1) * rows)
        keys = jnp.concatenate([anchor[k_at, :], own[k_at, :]], 0)
        values = jnp.concatenate([anchor[v_at, :], own[v_at, :]], 1)
        loads[g].wait()
        for h in range(share // HEAD):
            at = slice(g * share + h * HEAD, g * share + (h + 1) * HEAD)
            s = lax.dot_general(keys, q_buf[:, at], NT, preferred_element_type=F32)
            s = jnp.where(visible, s, HIDDEN)
            m = jnp.max(s, axis=0, keepdims=True)
            p = jnp.exp2((s - m) * SCALE)
            l = jnp.sum(p, axis=0, keepdims=True)
            a = jnp.dot(values, p.astype(BF16), preferred_element_type=F32)
            o_buf[:, at] = jnp.transpose(a * (alive / l)).astype(BF16)
        stores[g].start()
    for store in stores:
        store.wait()


def context_kernel(groups, rows, blocks, aliased, live_ref, q_ref, own, *refs):
    count = len(blocks)
    pieces, rest = refs[:count], refs[count + aliased :]
    o_ref, anchor, q_buf, o_buf, in_sems, out_sems = rest
    block = lax.axis_index("ctx")
    for b, piece in zip(blocks, pieces):

        @pl.when(block == b)
        def _():
            anchor[...] = piece[...]

    mine = functools.reduce(jnp.logical_or, [block == b for b in blocks])

    @pl.when(mine)
    def _():
        context_body(groups, rows, live_ref, q_ref, anchor, own, o_ref, q_buf, o_buf, in_sems, out_sems)


def context(live_blocks, q, own, anchors, groups, before=None):
    rows, width = q.shape
    blocks, pieces = zip(*anchors)
    extra = [] if before is None else [before]
    return pl.pallas_call(
        functools.partial(context_kernel, groups, rows, blocks, len(extra)),
        out_shape=jax.ShapeDtypeStruct(q.shape, q.dtype),
        in_specs=[scalar(), anywhere()] + [whole()] * (1 + len(pieces)) + [anywhere()] * len(extra),
        out_specs=anywhere(),
        input_output_aliases={3 + len(pieces): 0} if extra else {},
        scratch_shapes=[
            pltpu.VMEM(own.shape, own.dtype),
            pltpu.VMEM(q.shape, q.dtype),
            pltpu.VMEM(q.shape, q.dtype),
            pltpu.SemaphoreType.DMA((groups,)),
            pltpu.SemaphoreType.DMA((groups,)),
        ],
        compiler_params=LIMIT,
        name="context",
    )(live_blocks, q, own, *pieces, *extra)


def local(context_q, context_k, context_v, question_q, token_mask, live_blocks):
    n = lax.axis_size("ctx")
    rows, width = context_k.shape
    groups = width // HEAD
    ring = list(range(0, n, 2)) + list(range(n - 1, 0, -2))
    forth = [(ring[i], ring[(i + 1) % n]) for i in range(n)]
    back = [(b, a) for a, b in forth]

    own = pack(live_blocks, token_mask, context_k, context_v)
    half = n // 2
    left = right = own
    anchors = [(ring[0], own)]
    arrived = []
    for step in range(1, half + 1):
        left = lax.ppermute(left, "ctx", forth)
        late = [(ring[step], left)]
        if step < half:
            right = lax.ppermute(right, "ctx", back)
            late.append((ring[n - step], right))
        if step == 1:
            state = query_first(question_q, own, groups, rows)
        else:
            state = [state[0], *query_more(*state, arrived, groups, rows)]
        if step == half:
            context_output = context(live_blocks, context_q, own, anchors, groups)
        else:
            left, right, state = lax.optimization_barrier((left, right, state))
            late = [(late[0][0], left), (late[1][0], right)]
            arrived = [left, right]
            anchors += late
    query_output = query_last(*state, [left], groups, rows, jax.ShapeDtypeStruct(question_q.shape, BF16))
    context_output = context(live_blocks, context_q, own, late, groups, context_output)
    return context_output, query_output


def solution(mesh):
    rows = P(("dp", "ctx"), None)
    return jax.shard_map(
        local,
        mesh=mesh,
        in_specs=(rows, rows, rows, rows, P(("dp", "ctx")), P("dp")),
        out_specs=(rows, rows),
        check_vma=False,
    )
```

```python
import functools
import math

import jax
import jax.numpy as jnp
from jax import lax
from jax.experimental import pallas as pl
from jax.experimental.pallas import tpu as pltpu
from jax.sharding import PartitionSpec as P

HEAD = 128
FLAG_ROWS = 16
HIDDEN = -1e30
SCALE = HEAD**-0.5 / math.log(2.0)
NT = (((1,), (1,)), ((), ()))
F32 = jnp.float32
BF16 = jnp.bfloat16
LIMIT = pltpu.CompilerParams(vmem_limit_bytes=24 * 1024 * 1024)


def whole():
    return pl.BlockSpec(memory_space=pltpu.VMEM)


class Block:
    def __init__(self, refs, groups, rows):
        self.groups, self.rows = groups, rows
        self.k_ref, self.v_ref = refs[0], refs[-1]
        self.v_base = key_rows(groups, rows) if len(refs) == 1 else 0

    def keys(self, g):
        return self.k_ref[g * self.rows : (g + 1) * self.rows, :]

    def values(self, g):
        at = self.v_base + g * self.rows
        return jnp.transpose(self.v_ref[at : at + self.rows, :])

    def flag_rows(self):
        at = self.groups * self.rows
        return self.k_ref[at : at + FLAG_ROWS, :].astype(F32)

    def flags(self):
        return jnp.transpose(jnp.broadcast_to(self.flag_rows()[:1], (self.rows, self.rows)))

    def alive(self):
        return self.flag_rows()[FLAG_ROWS // 2 : FLAG_ROWS // 2 + 1]

    def seen(self, lanes):
        flags = self.flags()
        while flags.shape[1] < lanes:
            flags = jnp.concatenate([flags, flags], 1)
        return flags[:, :lanes] > 0.5


def outside():
    return pl.BlockSpec(memory_space=pltpu.HBM)


def key_rows(groups, rows):
    return groups * rows + FLAG_ROWS


def take(refs, parts, groups, rows):
    blocks, at = [], 0
    for count in parts:
        blocks.append(Block(refs[at : at + count], groups, rows))
        at += count
    return blocks, refs[at:]


def pack(live_blocks, token_mask, k, v):
    rows, width = k.shape
    groups = width // HEAD
    block = lax.axis_index("ctx")
    token = lax.broadcasted_iota(jnp.int32, (FLAG_ROWS, rows), 1)
    row = lax.broadcasted_iota(jnp.int32, (FLAG_ROWS, rows), 0)
    valid = (token_mask[None, :] != 0) | ((block == 0) & (token == 0)) | (row >= FLAG_ROWS // 2)
    flags = (valid & (block < live_blocks[0])).astype(BF16)

    def by_head(x):
        return x.reshape(rows, groups, HEAD).transpose(1, 0, 2).reshape(groups * rows, HEAD)

    return jnp.concatenate([by_head(k), flags, by_head(v)], 0)


def attend(block, g, q, seen):
    s = lax.dot_general(block.keys(g), q, NT, preferred_element_type=F32)
    s = jnp.where(seen, s, HIDDEN)
    m = jnp.max(s, axis=0, keepdims=True)
    p = jnp.exp2((s - m) * SCALE)
    l = jnp.sum(p, axis=0, keepdims=True)
    return m, l, jnp.dot(block.values(g), p.astype(BF16), preferred_element_type=F32)


def merge(one, two):
    top = jnp.maximum(one[0], two[0])
    f, h = jnp.exp2((one[0] - top) * SCALE), jnp.exp2((two[0] - top) * SCALE)
    return top, one[1] * f + two[1] * h, one[2] * f + two[2] * h


def load_state(acc_ref, stat_ref, g):
    return stat_ref[2 * g : 2 * g + 1, :], stat_ref[2 * g + 1 : 2 * g + 2, :], acc_ref[g * HEAD : (g + 1) * HEAD, :]


def store_state(acc_ref, stat_ref, g, state):
    stat_ref[2 * g : 2 * g + 1, :] = state[0]
    stat_ref[2 * g + 1 : 2 * g + 2, :] = state[1]
    acc_ref[g * HEAD : (g + 1) * HEAD, :] = state[2]


def first_kernel(groups, rows, q_ref, piece, stacked, acc, stat):
    n_q, width = q_ref.shape
    heads = width // HEAD // groups
    lanes = heads * n_q
    block = Block([piece], groups, rows)
    seen = block.seen(lanes)
    for g in range(groups):
        q = jnp.concatenate(
            [q_ref[:, (g * heads + h) * HEAD : (g * heads + h + 1) * HEAD].astype(F32) for h in range(heads)], 0
        ).astype(BF16)
        stacked[g * lanes : (g + 1) * lanes, :] = q
        store_state(acc, stat, g, attend(block, g, q, seen))


def state_shapes(groups, lanes):
    return [
        jax.ShapeDtypeStruct((groups * HEAD, lanes), F32),
        jax.ShapeDtypeStruct((2 * groups, lanes), F32),
    ]


def query_first(q, piece, groups, rows):
    n_q, width = q.shape
    lanes = n_q * width // HEAD // groups
    return pl.pallas_call(
        functools.partial(first_kernel, groups, rows),
        out_shape=[jax.ShapeDtypeStruct((groups * lanes, HEAD), BF16)] + state_shapes(groups, lanes),
        in_specs=[whole()] * 2,
        out_specs=[whole()] * 3,
        compiler_params=LIMIT,
        name="query_first",
    )(q, piece)


def more_kernel(groups, rows, parts, stacked, acc_in, stat_in, *refs):
    blocks, (acc, stat) = take(refs, parts, groups, rows)
    lanes = stacked.shape[0] // groups
    seen = [block.seen(lanes) for block in blocks]
    for g in range(groups):
        q = stacked[g * lanes : (g + 1) * lanes, :]
        state = load_state(acc_in, stat_in, g)
        for block, mask in zip(blocks, seen):
            state = merge(state, attend(block, g, q, mask))
        store_state(acc, stat, g, state)


def query_more(stacked, acc, stat, pieces, groups, rows):
    return pl.pallas_call(
        functools.partial(more_kernel, groups, rows, [len(piece) for piece in pieces]),
        out_shape=state_shapes(groups, stacked.shape[0] // groups),
        in_specs=[whole()] * (3 + sum(len(piece) for piece in pieces)),
        out_specs=[whole()] * 2,
        input_output_aliases={1: 0, 2: 1},
        compiler_params=LIMIT,
        name="query_more",
    )(stacked, acc, stat, *[part for piece in pieces for part in piece])


def context_body(groups, rows, resident, q_ref, anchor, own, o_ref, q_buf, o_buf, in_sems, out_sems):
    here = lax.axis_index("ctx")
    share = q_ref.shape[1] // groups
    spans = [pl.ds(g * share, share) for g in range(groups)]
    stores = [pltpu.make_async_copy(o_buf.at[:, at], o_ref.at[:, at], out_sems.at[g]) for g, at in enumerate(spans)]
    loads = []
    if not resident:
        loads = [pltpu.make_async_copy(q_ref.at[:, at], q_buf.at[:, at], in_sems.at[g]) for g, at in enumerate(spans)]
        q_ref = q_buf
    for load in loads:
        load.start()
    key = lax.broadcasted_iota(jnp.int32, (rows, rows), 0)
    row = lax.broadcasted_iota(jnp.int32, (rows, rows), 1)
    see_anchor = anchor.flags() * jnp.where(here > 0, 1.0, 0.0)
    see_own = jnp.where(key < row, own.flags(), jnp.where(key == row, 1.0, 0.0))
    visible = jnp.concatenate([see_anchor, see_own], 0) > 0.5
    alive = own.alive()
    for g in range(groups):
        keys = jnp.concatenate([anchor.keys(g), own.keys(g)], 0)
        values = jnp.concatenate([anchor.values(g), own.values(g)], 1)
        if loads:
            loads[g].wait()
        for h in range(share // HEAD):
            at = slice(g * share + h * HEAD, g * share + (h + 1) * HEAD)
            s = lax.dot_general(keys, q_ref[:, at], NT, preferred_element_type=F32)
            s = jnp.where(visible, s, HIDDEN)
            m = jnp.max(s, axis=0, keepdims=True)
            p = jnp.exp2((s - m) * SCALE)
            l = jnp.sum(p, axis=0, keepdims=True)
            a = jnp.dot(values, p.astype(BF16), preferred_element_type=F32)
            o_buf[:, at] = jnp.transpose(a * (alive / l)).astype(BF16)
        stores[g].start()
    for store in stores:
        store.wait()


def context_kernel(groups, rows, devices, parts, aliased, q_ref, own, *refs):
    blocks, rest = take(refs, parts, groups, rows)
    o_ref, anchor, *buffers = rest[aliased:]
    here = lax.axis_index("ctx")
    if len(blocks) == 1:
        first = blocks[0]
    else:
        first = Block([anchor], groups, rows)
        for device, block in zip(devices, blocks):

            @pl.when(here == device)
            def _():
                anchor[...] = block.k_ref[...]

    @pl.when(functools.reduce(jnp.logical_or, [here == device for device in devices]))
    def _():
        context_body(groups, rows, False, q_ref, first, Block([own], groups, rows), o_ref, *buffers)


def context(q, own, anchors, groups, before=None):
    rows, width = q.shape
    devices, pieces = zip(*anchors)
    parts = [len(piece) for piece in pieces]
    operands = [part for piece in pieces for part in piece]
    extra = [] if before is None else [before]
    return pl.pallas_call(
        functools.partial(context_kernel, groups, rows, devices, parts, len(extra)),
        out_shape=jax.ShapeDtypeStruct(q.shape, q.dtype),
        in_specs=[outside()] + [whole()] * (1 + len(operands)) + [outside()] * len(extra),
        out_specs=outside(),
        input_output_aliases={2 + len(operands): 0} if extra else {},
        scratch_shapes=[
            pltpu.VMEM(own.shape, own.dtype),
            pltpu.VMEM(q.shape, q.dtype),
            pltpu.VMEM(q.shape, q.dtype),
            pltpu.SemaphoreType.DMA((groups,)),
            pltpu.SemaphoreType.DMA((groups,)),
        ],
        compiler_params=LIMIT,
        name="context",
    )(q, own, *operands, *extra)


def finish_kernel(
    groups, rows, device, parts, stacked, acc, stat, q_ref, own, *refs
):
    (block,), rest = take(refs, parts, groups, rows)
    _, query_ref, context_ref, buffer, out_sems, *buffers = rest
    lanes = stacked.shape[0] // groups
    n_q, width = buffer.shape
    heads = width // HEAD // groups
    share = heads * HEAD
    spans = [pl.ds(g * share, share) for g in range(groups)]
    stores = [
        pltpu.make_async_copy(buffer.at[:, at], query_ref.at[:, at], out_sems.at[g]) for g, at in enumerate(spans)
    ]
    seen = block.seen(lanes)
    for g in range(groups):
        q = stacked[g * lanes : (g + 1) * lanes, :]
        _, total, part = merge(load_state(acc, stat, g), attend(block, g, q, seen))
        out = jnp.transpose(part / total)
        for h in range(heads):
            at = g * share + h * HEAD
            buffer[:, at : at + HEAD] = out[h * n_q : (h + 1) * n_q].astype(BF16)
        stores[g].start()

    @pl.when(lax.axis_index("ctx") == device)
    def _():
        context_body(groups, rows, True, q_ref, block, Block([own], groups, rows), context_ref, *buffers)

    for store in stores:
        store.wait()


def finish(stacked, acc, stat, q, own, last, groups, shape, before):
    rows, width = q.shape
    device, piece = last
    return pl.pallas_call(
        functools.partial(finish_kernel, groups, rows, device, [len(piece)]),
        out_shape=[shape, jax.ShapeDtypeStruct(q.shape, q.dtype)],
        in_specs=[whole()] * (5 + len(piece)) + [outside()],
        out_specs=[outside()] * 2,
        input_output_aliases={5 + len(piece): 1},
        scratch_shapes=[
            pltpu.VMEM(shape.shape, shape.dtype),
            pltpu.SemaphoreType.DMA((groups,)),
            pltpu.VMEM((FLAG_ROWS, HEAD), q.dtype),
            pltpu.VMEM(q.shape, q.dtype),
            pltpu.SemaphoreType.DMA((groups,)),
            pltpu.SemaphoreType.DMA((groups,)),
        ],
        compiler_params=LIMIT,
        name="finish",
    )(stacked, acc, stat, q, own, *piece, before)


def local(context_q, context_k, context_v, question_q, token_mask, live_blocks):
    n = lax.axis_size("ctx")
    rows, width = context_k.shape
    groups = width // HEAD
    ring = list(range(0, n, 2)) + list(range(n - 1, 0, -2))
    forth = [(ring[i], ring[(i + 1) % n]) for i in range(n)]
    back = [(b, a) for a, b in forth]

    own = pack(live_blocks, token_mask, context_k, context_v)
    half = n // 2
    split = key_rows(groups, rows)
    left = right = own
    arrived = [(ring[0], (own,))]
    context_output = state = None
    for step in range(1, half + 1):
        if step < half:
            left = lax.ppermute(left, "ctx", forth)
            right = lax.ppermute(right, "ctx", back)
        else:
            left = lax.ppermute(left[:split], "ctx", forth)
            right = lax.ppermute(right[split:], "ctx", back)
        pieces = [piece for _, piece in arrived]
        if state is None:
            state = query_first(question_q, own, groups, rows)
        else:
            state = [state[0], *query_more(*state, pieces, groups, rows)]
        context_output = context(context_q, own, arrived, groups, context_output)
        if step < half:
            left = lax.optimization_barrier((left, state, context_output))[0]
            right, state, context_output = lax.optimization_barrier((right, state, context_output))
            arrived = [(ring[step], (left,)), (ring[n - step], (right,))]
    query_output, context_output = finish(
        *state,
        context_q,
        own,
        (ring[half], (left, right)),
        groups,
        jax.ShapeDtypeStruct(question_q.shape, BF16),
        context_output,
    )
    return context_output, query_output


def solution(mesh):
    rows = P(("dp", "ctx"), None)
    return jax.shard_map(
        local,
        mesh=mesh,
        in_specs=(rows, rows, rows, rows, P(("dp", "ctx")), P("dp")),
        out_specs=(rows, rows),
        check_vma=False,
    )
```

```python
import functools
import math

import jax
import jax.numpy as jnp
from jax import lax
from jax.experimental import pallas as pl
from jax.experimental.pallas import tpu as pltpu
from jax.sharding import PartitionSpec as P

HEAD = 128
FLAG_ROWS = 16
HIDDEN = -1e30
SCALE = HEAD**-0.5 / math.log(2.0)
NT = (((1,), (1,)), ((), ()))
F32 = jnp.float32
BF16 = jnp.bfloat16
LIMIT = pltpu.CompilerParams(vmem_limit_bytes=24 * 1024 * 1024)


def whole():
    return pl.BlockSpec(memory_space=pltpu.VMEM)


class Block:
    def __init__(self, refs, groups, rows):
        self.groups, self.rows = groups, rows
        self.k_ref, self.v_ref = refs[0], refs[-1]
        self.v_base = groups * rows if len(refs) == 1 else 0

    def keys(self, g):
        if self.k_ref.shape[1] > HEAD:
            return self.k_ref[:, g * HEAD : (g + 1) * HEAD]
        return self.k_ref[g * self.rows : (g + 1) * self.rows, :]

    def values(self, g):
        at = self.v_base + g * self.rows
        return jnp.transpose(self.v_ref[at : at + self.rows, :])

    def flag_rows(self):
        at = self.v_base + self.groups * self.rows
        return self.v_ref[at : at + FLAG_ROWS, :].astype(F32)

    def flags(self):
        return jnp.transpose(jnp.broadcast_to(self.flag_rows()[:1], (self.rows, self.rows)))

    def alive(self):
        return self.flag_rows()[FLAG_ROWS // 2 : FLAG_ROWS // 2 + 1]

    def seen(self, lanes):
        flags = self.flags()
        while flags.shape[1] < lanes:
            flags = jnp.concatenate([flags, flags], 1)
        return flags[:, :lanes] > 0.5


def outside():
    return pl.BlockSpec(memory_space=pltpu.HBM)


def take(refs, parts, groups, rows):
    blocks, at = [], 0
    for count in parts:
        blocks.append(Block(refs[at : at + count], groups, rows))
        at += count
    return blocks, refs[at:]


def pack(live_blocks, token_mask, v):
    rows, width = v.shape
    groups = width // HEAD
    block = lax.axis_index("ctx")
    token = lax.broadcasted_iota(jnp.int32, (FLAG_ROWS, rows), 1)
    row = lax.broadcasted_iota(jnp.int32, (FLAG_ROWS, rows), 0)
    valid = (token_mask[None, :] != 0) | ((block == 0) & (token == 0)) | (row >= FLAG_ROWS // 2)
    flags = (valid & (block < live_blocks[0])).astype(BF16)
    by_head = v.reshape(rows, groups, HEAD).transpose(1, 0, 2).reshape(groups * rows, HEAD)
    return jnp.concatenate([by_head, flags], 0)


def attend(block, g, q, seen):
    s = lax.dot_general(block.keys(g), q, NT, preferred_element_type=F32)
    s = jnp.where(seen, s, HIDDEN)
    m = jnp.max(s, axis=0, keepdims=True)
    p = jnp.exp2((s - m) * SCALE)
    l = jnp.sum(p, axis=0, keepdims=True)
    return m, l, jnp.dot(block.values(g), p.astype(BF16), preferred_element_type=F32)


def merge(one, two):
    top = jnp.maximum(one[0], two[0])
    f, h = jnp.exp2((one[0] - top) * SCALE), jnp.exp2((two[0] - top) * SCALE)
    return top, one[1] * f + two[1] * h, one[2] * f + two[2] * h


def load_state(acc_ref, stat_ref, g):
    return stat_ref[2 * g : 2 * g + 1, :], stat_ref[2 * g + 1 : 2 * g + 2, :], acc_ref[g * HEAD : (g + 1) * HEAD, :]


def store_state(acc_ref, stat_ref, g, state):
    stat_ref[2 * g : 2 * g + 1, :] = state[0]
    stat_ref[2 * g + 1 : 2 * g + 2, :] = state[1]
    acc_ref[g * HEAD : (g + 1) * HEAD, :] = state[2]


def first_kernel(groups, rows, q_ref, k_ref, v_ref, stacked, acc, stat):
    n_q, width = q_ref.shape
    heads = width // HEAD // groups
    lanes = heads * n_q
    block = Block([k_ref, v_ref], groups, rows)
    seen = block.seen(lanes)
    for g in range(groups):
        q = jnp.concatenate(
            [q_ref[:, (g * heads + h) * HEAD : (g * heads + h + 1) * HEAD].astype(F32) for h in range(heads)], 0
        ).astype(BF16)
        stacked[g * lanes : (g + 1) * lanes, :] = q
        store_state(acc, stat, g, attend(block, g, q, seen))


def state_shapes(groups, lanes):
    return [
        jax.ShapeDtypeStruct((groups * HEAD, lanes), F32),
        jax.ShapeDtypeStruct((2 * groups, lanes), F32),
    ]


def query_first(q, k, v, groups, rows):
    n_q, width = q.shape
    lanes = n_q * width // HEAD // groups
    return pl.pallas_call(
        functools.partial(first_kernel, groups, rows),
        out_shape=[jax.ShapeDtypeStruct((groups * lanes, HEAD), BF16)] + state_shapes(groups, lanes),
        in_specs=[whole()] * 3,
        out_specs=[whole()] * 3,
        cost_estimate=pl.CostEstimate(flops=0, bytes_accessed=0, transcendentals=0),
        compiler_params=LIMIT,
        name="query_first",
    )(q, k, v)


def more_kernel(groups, rows, parts, stacked, acc_in, stat_in, *refs):
    blocks, (acc, stat) = take(refs, parts, groups, rows)
    lanes = stacked.shape[0] // groups
    seen = [block.seen(lanes) for block in blocks]
    for g in range(groups):
        q = stacked[g * lanes : (g + 1) * lanes, :]
        state = load_state(acc_in, stat_in, g)
        for block, mask in zip(blocks, seen):
            state = merge(state, attend(block, g, q, mask))
        store_state(acc, stat, g, state)


def query_more(stacked, acc, stat, pieces, groups, rows):
    return pl.pallas_call(
        functools.partial(more_kernel, groups, rows, [len(piece) for piece in pieces]),
        out_shape=state_shapes(groups, stacked.shape[0] // groups),
        in_specs=[whole()] * (3 + sum(len(piece) for piece in pieces)),
        out_specs=[whole()] * 2,
        input_output_aliases={1: 0, 2: 1},
        compiler_params=LIMIT,
        name="query_more",
    )(stacked, acc, stat, *[part for piece in pieces for part in piece])


def context_body(groups, rows, q_ref, anchor, own, o_ref, o_buf, out_sems):
    here = lax.axis_index("ctx")
    share = q_ref.shape[1] // groups
    spans = [pl.ds(g * share, share) for g in range(groups)]
    stores = [pltpu.make_async_copy(o_buf.at[:, at], o_ref.at[:, at], out_sems.at[g]) for g, at in enumerate(spans)]
    key = lax.broadcasted_iota(jnp.int32, (rows, rows), 0)
    row = lax.broadcasted_iota(jnp.int32, (rows, rows), 1)
    see_anchor = anchor.flags() * jnp.where(here > 0, 1.0, 0.0)
    see_own = jnp.where(key < row, own.flags(), jnp.where(key == row, 1.0, 0.0))
    visible = jnp.concatenate([see_anchor, see_own], 0) > 0.5
    alive = own.alive()
    for g in range(groups):
        keys = jnp.concatenate([anchor.keys(g), own.keys(g)], 0)
        values = jnp.concatenate([anchor.values(g), own.values(g)], 1)
        for h in range(share // HEAD):
            at = slice(g * share + h * HEAD, g * share + (h + 1) * HEAD)
            s = lax.dot_general(keys, q_ref[:, at], NT, preferred_element_type=F32)
            s = jnp.where(visible, s, HIDDEN)
            m = jnp.max(s, axis=0, keepdims=True)
            p = jnp.exp2((s - m) * SCALE)
            l = jnp.sum(p, axis=0, keepdims=True)
            a = jnp.dot(values, p.astype(BF16), preferred_element_type=F32)
            o_buf[:, at] = jnp.transpose(a * (alive / l)).astype(BF16)
        stores[g].start()
    for store in stores:
        store.wait()


def context_kernel(groups, rows, devices, parts, aliased, q_ref, own_k, own_v, *refs):
    blocks, rest = take(refs, parts, groups, rows)
    o_ref, anchor_k, anchor_v, *buffers = rest[aliased:]
    here = lax.axis_index("ctx")
    first = Block([anchor_k, anchor_v], groups, rows)
    for device, block in zip(devices, blocks):

        @pl.when(here == device)
        def _():
            anchor_k[...] = block.k_ref[...]
            anchor_v[...] = block.v_ref[...]

    @pl.when(functools.reduce(jnp.logical_or, [here == device for device in devices]))
    def _():
        context_body(groups, rows, q_ref, first, Block([own_k, own_v], groups, rows), o_ref, *buffers)


def context(q, own, anchors, groups, before=None):
    rows, width = q.shape
    devices, pieces = zip(*anchors)
    parts = [len(piece) for piece in pieces]
    operands = [part for piece in pieces for part in piece]
    extra = [] if before is None else [before]
    return pl.pallas_call(
        functools.partial(context_kernel, groups, rows, devices, parts, len(extra)),
        out_shape=jax.ShapeDtypeStruct(q.shape, q.dtype),
        in_specs=[whole()] * (3 + len(operands)) + [outside()] * len(extra),
        out_specs=outside(),
        input_output_aliases={3 + len(operands): 0} if extra else {},
        scratch_shapes=[
            pltpu.VMEM(own[0].shape, BF16),
            pltpu.VMEM(own[1].shape, BF16),
            pltpu.VMEM(q.shape, q.dtype),
            pltpu.SemaphoreType.DMA((groups,)),
        ],
        compiler_params=LIMIT,
        name="context",
    )(q, *own, *operands, *extra)


def finish_kernel(
    groups, rows, device, parts, stacked, acc, stat, q_ref, own_k, own_v, *refs
):
    (block,), rest = take(refs, parts, groups, rows)
    _, query_ref, context_ref, buffer, out_sems, *buffers = rest
    lanes = stacked.shape[0] // groups
    n_q, width = buffer.shape
    heads = width // HEAD // groups
    share = heads * HEAD
    spans = [pl.ds(g * share, share) for g in range(groups)]
    stores = [
        pltpu.make_async_copy(buffer.at[:, at], query_ref.at[:, at], out_sems.at[g]) for g, at in enumerate(spans)
    ]
    seen = block.seen(lanes)
    for g in range(groups):
        q = stacked[g * lanes : (g + 1) * lanes, :]
        _, total, part = merge(load_state(acc, stat, g), attend(block, g, q, seen))
        out = jnp.transpose(part / total)
        for h in range(heads):
            at = g * share + h * HEAD
            buffer[:, at : at + HEAD] = out[h * n_q : (h + 1) * n_q].astype(BF16)
        stores[g].start()

    @pl.when(lax.axis_index("ctx") == device)
    def _():
        context_body(groups, rows, q_ref, block, Block([own_k, own_v], groups, rows), context_ref, *buffers)

    for store in stores:
        store.wait()


def finish(stacked, acc, stat, q, own, last, groups, shape, before):
    rows, width = q.shape
    device, piece = last
    return pl.pallas_call(
        functools.partial(finish_kernel, groups, rows, device, [len(piece)]),
        out_shape=[shape, jax.ShapeDtypeStruct(q.shape, q.dtype)],
        in_specs=[whole()] * (6 + len(piece)) + [outside()],
        out_specs=[outside()] * 2,
        input_output_aliases={6 + len(piece): 1},
        scratch_shapes=[
            pltpu.VMEM(shape.shape, shape.dtype),
            pltpu.SemaphoreType.DMA((groups,)),
            pltpu.VMEM(q.shape, q.dtype),
            pltpu.SemaphoreType.DMA((groups,)),
        ],
        compiler_params=LIMIT,
        name="finish",
    )(stacked, acc, stat, q, *own, *piece, before)


def local(context_q, context_k, context_v, question_q, token_mask, live_blocks):
    n = lax.axis_size("ctx")
    rows, width = context_k.shape
    groups = width // HEAD
    ring = list(range(0, n, 2)) + list(range(n - 1, 0, -2))
    forth = [(ring[i], ring[(i + 1) % n]) for i in range(n)]
    back = [(b, a) for a, b in forth]

    half = n // 2

    def send(value, pairs):
        return lax.ppermute(value, "ctx", pairs)

    packed = pack(live_blocks, token_mask, context_v)
    own = (context_k, packed)
    left_k = right_k = context_k
    left_v = right_v = packed
    state = None
    arrived, anchors = [], [(ring[0], own)]
    for step in range(1, half + 1):
        left_k, right_v = send(left_k, forth), send(right_v, back)
        if step < half:
            left_v, right_k = send(left_v, forth), send(right_k, back)
        if step == 1:
            state = query_first(question_q, *own, groups, rows)
        else:
            state = [state[0], *query_more(*state, [piece for _, piece in arrived], groups, rows)]
        if step < half:
            right_k, state = lax.optimization_barrier((right_k, state))
            arrived = [(ring[step], (left_k, left_v)), (ring[n - step], (right_k, right_v))]
        if step < half - 1:
            anchors += arrived
    context_output = context(context_q, own, anchors, groups)
    context_output = context(context_q, own, arrived, groups, context_output)
    left, right = left_k, right_v
    query_output, context_output = finish(
        *state,
        context_q,
        own,
        (ring[half], (left, right)),
        groups,
        jax.ShapeDtypeStruct(question_q.shape, BF16),
        context_output,
    )
    return context_output, query_output


def solution(mesh):
    rows = P(("dp", "ctx"), None)
    return jax.shard_map(
        local,
        mesh=mesh,
        in_specs=(rows, rows, rows, rows, P(("dp", "ctx")), P("dp")),
        out_specs=(rows, rows),
        check_vma=False,
    )
```

```python
import functools
import math

import jax
import jax.numpy as jnp
from jax import lax
from jax.experimental import pallas as pl
from jax.experimental.pallas import tpu as pltpu
from jax.sharding import PartitionSpec as P

HEAD = 128
FLAG_ROWS = 16
HIDDEN = -1e30
SCALE = HEAD**-0.5 / math.log(2.0)
NT = (((1,), (1,)), ((), ()))
F32 = jnp.float32
BF16 = jnp.bfloat16
LIMIT = pltpu.CompilerParams(vmem_limit_bytes=24 * 1024 * 1024)


def whole():
    return pl.BlockSpec(memory_space=pltpu.VMEM)


class Block:
    def __init__(self, refs, groups, rows):
        self.groups, self.rows = groups, rows
        self.k_ref, self.v_ref = refs[0], refs[-1]
        self.v_base = groups * rows if len(refs) == 1 else 0

    def keys(self, g):
        if self.k_ref.shape[1] > HEAD:
            return self.k_ref[:, g * HEAD : (g + 1) * HEAD]
        return self.k_ref[g * self.rows : (g + 1) * self.rows, :]

    def values(self, g):
        at = self.v_base + g * self.rows
        return jnp.transpose(self.v_ref[at : at + self.rows, :])

    def flags(self):
        at = self.v_base + self.groups * self.rows
        flags = self.v_ref[at : at + FLAG_ROWS, :].astype(F32)[:1]
        return jnp.transpose(jnp.broadcast_to(flags, (self.rows, self.rows)))

    def bias(self, lanes, alive):
        flags = self.flags()
        while flags.shape[1] < lanes:
            flags = jnp.concatenate([flags, flags], 1)
        return jnp.where(flags[:, :lanes] > jnp.where(alive, 0.5, 2.0), 0.0, HIDDEN)


def scalar():
    return pl.BlockSpec(memory_space=pltpu.SMEM)


def ring_device(n, shift):
    here = lax.axis_index("ctx")
    place = jnp.where(lax.rem(here, 2) == 0, lax.div(here, 2), n - 1 - lax.div(here, 2))
    place = lax.rem(place + shift + n, n)
    return jnp.where(place < n // 2, 2 * place, 2 * (n - 1 - place) + 1)


def outside():
    return pl.BlockSpec(memory_space=pltpu.HBM)


def take(refs, parts, groups, rows):
    blocks, at = [], 0
    for count in parts:
        blocks.append(Block(refs[at : at + count], groups, rows))
        at += count
    return blocks, refs[at:]


def pack(token_mask, v):
    rows, width = v.shape
    groups = width // HEAD
    block = lax.axis_index("ctx")
    token = lax.broadcasted_iota(jnp.int32, (FLAG_ROWS, rows), 1)
    flags = ((token_mask[None, :] != 0) | ((block == 0) & (token == 0))).astype(BF16)
    by_head = v.reshape(rows, groups, HEAD).transpose(1, 0, 2).reshape(groups * rows, HEAD)
    return jnp.concatenate([by_head, flags], 0)


def attend(blocks, g, q, biases):
    keys = jnp.concatenate([block.keys(g) for block in blocks], 0)
    scores = lax.dot_general(keys, q, NT, preferred_element_type=F32)
    results = []
    for i, (block, bias) in enumerate(zip(blocks, biases)):
        s = scores[i * block.rows : (i + 1) * block.rows] + bias
        m = jnp.max(s, axis=0, keepdims=True)
        p = jnp.exp2((s - m) * SCALE)
        l = jnp.sum(p, axis=0, keepdims=True)
        results.append((m, l, jnp.dot(block.values(g), p.astype(BF16), preferred_element_type=F32)))
    return results


def merge(parts):
    top = functools.reduce(jnp.maximum, [m for m, _, _ in parts])
    factors = [jnp.exp2((m - top) * SCALE) for m, _, _ in parts]
    total = sum(l * f for (_, l, _), f in zip(parts, factors))
    return top, total, sum(a * f for (_, _, a), f in zip(parts, factors))


def load_state(acc_ref, stat_ref, g, at):
    rows = slice(g * HEAD, (g + 1) * HEAD)
    return stat_ref[2 * g : 2 * g + 1, at], stat_ref[2 * g + 1 : 2 * g + 2, at], acc_ref[rows, at]


def store_state(acc_ref, stat_ref, g, at, state):
    stat_ref[2 * g : 2 * g + 1, at] = state[0]
    stat_ref[2 * g + 1 : 2 * g + 2, at] = state[1]
    acc_ref[g * HEAD : (g + 1) * HEAD, at] = state[2]


def first_kernel(groups, rows, live_ref, q_ref, k_ref, v_ref, stacked, acc, stat):
    n_q, width = q_ref.shape
    heads = width // HEAD // groups
    lanes = heads * n_q
    block = Block([k_ref, v_ref], groups, rows)
    bias = block.bias(lanes, lax.axis_index("ctx") < live_ref[0])
    for g in range(groups):
        q = jnp.concatenate(
            [q_ref[:, (g * heads + h) * HEAD : (g * heads + h + 1) * HEAD].astype(F32) for h in range(heads)], 0
        ).astype(BF16)
        stacked[g * lanes : (g + 1) * lanes, :] = q
        store_state(acc, stat, g, slice(None), attend([block], g, q, [bias])[0])


def state_shapes(groups, lanes):
    return [
        jax.ShapeDtypeStruct((groups * HEAD, lanes), F32),
        jax.ShapeDtypeStruct((2 * groups, lanes), F32),
    ]


def query_first(live_blocks, q, k, v, groups, rows):
    n_q, width = q.shape
    lanes = n_q * width // HEAD // groups
    return pl.pallas_call(
        functools.partial(first_kernel, groups, rows),
        out_shape=[jax.ShapeDtypeStruct((groups * lanes, HEAD), BF16)] + state_shapes(groups, lanes),
        in_specs=[scalar()] + [whole()] * 3,
        out_specs=[whole()] * 3,
        cost_estimate=pl.CostEstimate(flops=0, bytes_accessed=0, transcendentals=0),
        compiler_params=LIMIT,
        name="query_first",
    )(live_blocks, q, k, v)


def query_body(blocks, shifts, n, live_ref, groups, stacked, acc_in, stat_in, acc, stat):
    lanes = stacked.shape[0] // groups
    step = min(lanes, HEAD)
    biases = [block.bias(step, ring_device(n, shift) < live_ref[0]) for block, shift in zip(blocks, shifts)]
    for g in range(groups):
        for first in range(0, lanes, step):
            at = slice(first, first + step)
            q = stacked[g * lanes + first : g * lanes + first + step, :]
            parts = [load_state(acc_in, stat_in, g, at)] + attend(blocks, g, q, biases)
            store_state(acc, stat, g, at, merge(parts))


def more_kernel(groups, rows, parts, shifts, n, live_ref, stacked, acc_in, stat_in, *refs):
    blocks, (acc, stat) = take(refs, parts, groups, rows)
    query_body(blocks, shifts, n, live_ref, groups, stacked, acc_in, stat_in, acc, stat)


def query_more(live_blocks, stacked, acc, stat, pieces, shifts, n, groups, rows):
    operands = [part for piece in pieces for part in piece]
    return pl.pallas_call(
        functools.partial(more_kernel, groups, rows, [len(piece) for piece in pieces], shifts, n),
        out_shape=state_shapes(groups, stacked.shape[0] // groups),
        in_specs=[scalar()] + [whole()] * (3 + len(operands)),
        out_specs=[whole()] * 2,
        input_output_aliases={2: 0, 3: 1},
        compiler_params=LIMIT,
        name="query_more",
    )(live_blocks, stacked, acc, stat, *operands)


def context_body(groups, rows, live_ref, q_ref, anchor, own, o_ref, o_buf, out_sems):
    here = lax.axis_index("ctx")
    share = q_ref.shape[1] // groups
    spans = [pl.ds(g * share, share) for g in range(groups)]
    stores = [pltpu.make_async_copy(o_buf.at[:, at], o_ref.at[:, at], out_sems.at[g]) for g, at in enumerate(spans)]
    key = lax.broadcasted_iota(jnp.int32, (rows, rows), 0)
    row = lax.broadcasted_iota(jnp.int32, (rows, rows), 1)
    see_anchor = anchor.flags() * jnp.where(here > 0, 1.0, 0.0)
    see_own = jnp.where(key < row, own.flags(), jnp.where(key == row, 1.0, 0.0))
    bias = jnp.where(jnp.concatenate([see_anchor, see_own], 0) > 0.5, 0.0, HIDDEN)
    alive = jnp.where(here < live_ref[0], 1.0, 0.0)
    for g in range(groups):
        keys = jnp.concatenate([anchor.keys(g), own.keys(g)], 0)
        values = jnp.concatenate([anchor.values(g), own.values(g)], 1)
        for h in range(share // HEAD):
            at = slice(g * share + h * HEAD, g * share + (h + 1) * HEAD)
            s = lax.dot_general(keys, q_ref[:, at], NT, preferred_element_type=F32)
            s = s + bias
            m = jnp.max(s, axis=0, keepdims=True)
            p = jnp.exp2((s - m) * SCALE)
            l = jnp.sum(p, axis=0, keepdims=True)
            a = jnp.dot(values, p.astype(BF16), preferred_element_type=F32)
            o_buf[:, at] = jnp.transpose((a * (alive / l)).astype(BF16))
        stores[g].start()
    return stores


def both_kernel(groups, rows, devices, parts, shifts, n, aliased, live_ref, stacked, acc_in, stat_in, q_ref, own_k, own_v, *refs):
    blocks, rest = take(refs, parts, groups, rows)
    acc, stat, o_ref, anchor_k, anchor_v, o_buf, out_sems = rest[aliased:]
    here = lax.axis_index("ctx")
    for device, block in zip(devices, blocks):

        @pl.when(here == device)
        def _():
            anchor_k[...] = block.k_ref[...]
            anchor_v[...] = block.v_ref[...]

    mine = functools.reduce(jnp.logical_or, [here == device for device in devices])
    first, own = Block([anchor_k, anchor_v], groups, rows), Block([own_k, own_v], groups, rows)

    @pl.when(mine)
    def _():
        stores = context_body(groups, rows, live_ref, q_ref, first, own, o_ref, o_buf, out_sems)
        query_body(blocks[-len(shifts) :], shifts, n, live_ref, groups, stacked, acc_in, stat_in, acc, stat)
        for store in stores:
            store.wait()

    @pl.when(jnp.logical_not(mine))
    def _():
        query_body(blocks[-len(shifts) :], shifts, n, live_ref, groups, stacked, acc_in, stat_in, acc, stat)


def both(live_blocks, stacked, acc, stat, q, own, anchors, shifts, n, groups, before=None):
    rows = own[0].shape[0]
    devices, pieces = zip(*anchors)
    parts = [len(piece) for piece in pieces]
    operands = [part for piece in pieces for part in piece]
    extra = [] if before is None else [before]
    return pl.pallas_call(
        functools.partial(both_kernel, groups, rows, devices, parts, shifts, n, len(extra)),
        out_shape=state_shapes(groups, stacked.shape[0] // groups) + [jax.ShapeDtypeStruct(q.shape, q.dtype)],
        in_specs=[scalar()] + [whole()] * (6 + len(operands)) + [outside()] * len(extra),
        out_specs=[whole()] * 2 + [outside()],
        input_output_aliases={2: 0, 3: 1} | ({7 + len(operands): 2} if extra else {}),
        scratch_shapes=[
            pltpu.VMEM(own[0].shape, BF16),
            pltpu.VMEM(own[1].shape, BF16),
            pltpu.VMEM(q.shape, q.dtype),
            pltpu.SemaphoreType.DMA((groups,)),
        ],
        compiler_params=LIMIT,
        name="both",
    )(live_blocks, stacked, acc, stat, q, *own, *operands, *extra)


def finish_kernel(
    groups, rows, device, parts, n, live_ref, stacked, acc, stat, q_ref, own_k, own_v, *refs
):
    (block,), rest = take(refs, parts, groups, rows)
    _, query_ref, context_ref, buffer, out_sems, *buffers = rest
    lanes = stacked.shape[0] // groups
    n_q, width = buffer.shape
    heads = width // HEAD // groups
    share = heads * HEAD
    spans = [pl.ds(g * share, share) for g in range(groups)]
    stores = [
        pltpu.make_async_copy(buffer.at[:, at], query_ref.at[:, at], out_sems.at[g]) for g, at in enumerate(spans)
    ]
    bias = block.bias(lanes, ring_device(n, n // 2) < live_ref[0])
    for g in range(groups):
        q = stacked[g * lanes : (g + 1) * lanes, :]
        state = load_state(acc, stat, g, slice(None))
        _, total, part = merge([state] + attend([block], g, q, [bias]))
        out = jnp.transpose(part / total)
        for h in range(heads):
            at = g * share + h * HEAD
            buffer[:, at : at + HEAD] = out[h * n_q : (h + 1) * n_q].astype(BF16)
        stores[g].start()

    @pl.when(lax.axis_index("ctx") == device)
    def _():
        own = Block([own_k, own_v], groups, rows)
        for store in context_body(groups, rows, live_ref, q_ref, block, own, context_ref, *buffers):
            store.wait()

    for store in stores:
        store.wait()


def finish(live_blocks, stacked, acc, stat, q, own, last, n, groups, shape, before):
    rows, width = q.shape
    device, piece = last
    return pl.pallas_call(
        functools.partial(finish_kernel, groups, rows, device, [len(piece)], n),
        out_shape=[shape, jax.ShapeDtypeStruct(q.shape, q.dtype)],
        in_specs=[scalar()] + [whole()] * (6 + len(piece)) + [outside()],
        out_specs=[outside()] * 2,
        input_output_aliases={7 + len(piece): 1},
        scratch_shapes=[
            pltpu.VMEM(shape.shape, shape.dtype),
            pltpu.SemaphoreType.DMA((groups,)),
            pltpu.VMEM(q.shape, q.dtype),
            pltpu.SemaphoreType.DMA((groups,)),
        ],
        compiler_params=LIMIT,
        name="finish",
    )(live_blocks, stacked, acc, stat, q, *own, *piece, before)


def local(context_q, context_k, context_v, question_q, token_mask, live_blocks):
    n = lax.axis_size("ctx")
    rows, width = context_k.shape
    groups = width // HEAD
    ring = list(range(0, n, 2)) + list(range(n - 1, 0, -2))
    forth = [(ring[i], ring[(i + 1) % n]) for i in range(n)]
    back = [(b, a) for a, b in forth]

    half = n // 2

    def send(value, pairs):
        return lax.ppermute(value, "ctx", pairs)

    packed = pack(token_mask, context_v)
    own = (context_k, packed)
    left_k = right_k = context_k
    left_v = right_v = packed
    state = context_output = None
    arrived, anchors = [], [(ring[0], own)]
    for step in range(1, half + 1):
        left_k, right_v = send(left_k, forth), send(right_v, back)
        if step < half:
            left_v, right_k = send(left_v, forth), send(right_k, back)
        pieces = [piece for _, piece in arrived]
        if step == 1:
            state = query_first(live_blocks, question_q, *own, groups, rows)
        elif step < half - 1:
            state = [state[0], *query_more(live_blocks, *state, pieces, (1 - step, step - 1), n, groups, rows)]
        else:
            new = anchors + arrived if step == half - 1 else arrived
            *update, context_output = both(
                live_blocks, *state, context_q, own, new, (1 - step, step - 1), n, groups, context_output
            )
            state = [state[0], *update]
        anchors += arrived
        if step < half:
            right_k, state = lax.optimization_barrier((right_k, state))
            arrived = [(ring[step], (left_k, left_v)), (ring[n - step], (right_k, right_v))]
    left, right = left_k, right_v
    query_output, context_output = finish(
        live_blocks,
        *state,
        context_q,
        own,
        (ring[half], (left, right)),
        n,
        groups,
        jax.ShapeDtypeStruct(question_q.shape, BF16),
        context_output,
    )
    return context_output, query_output


def solution(mesh):
    rows = P(("dp", "ctx"), None)
    return jax.shard_map(
        local,
        mesh=mesh,
        in_specs=(rows, rows, rows, rows, P(("dp", "ctx")), P("dp")),
        out_specs=(rows, rows),
        check_vma=False,
    )
```

```python
import functools
import math

import jax
import jax.numpy as jnp
from jax import lax
from jax.experimental import pallas as pl
from jax.experimental.pallas import tpu as pltpu
from jax.sharding import PartitionSpec as P

HEAD = 128
FLAG_ROWS = 16
HIDDEN = -1e30
SCALE = HEAD**-0.5 / math.log(2.0)
NT = (((1,), (1,)), ((), ()))
F32 = jnp.float32
BF16 = jnp.bfloat16
LIMIT = pltpu.CompilerParams(vmem_limit_bytes=24 * 1024 * 1024)


def whole():
    return pl.BlockSpec(memory_space=pltpu.VMEM)


class Block:
    def __init__(self, refs, groups, rows):
        self.groups, self.rows = groups, rows
        self.k_ref, self.v_ref = refs[0], refs[-1]
        self.v_base = groups * rows if len(refs) == 1 else 0

    def keys(self, g):
        if self.k_ref.shape[1] > HEAD:
            return self.k_ref[:, g * HEAD : (g + 1) * HEAD]
        return self.k_ref[g * self.rows : (g + 1) * self.rows, :]

    def values(self, g):
        at = self.v_base + g * self.rows
        return jnp.transpose(self.v_ref[at : at + self.rows, :])

    def flags(self):
        at = self.v_base + self.groups * self.rows
        flags = self.v_ref[at : at + FLAG_ROWS, :].astype(F32)[:1]
        return jnp.transpose(jnp.broadcast_to(flags, (self.rows, self.rows)))

    def bias(self, lanes, alive):
        flags = self.flags()
        while flags.shape[1] < lanes:
            flags = jnp.concatenate([flags, flags], 1)
        return jnp.where(flags[:, :lanes] > jnp.where(alive, 0.5, 2.0), 0.0, HIDDEN)


def scalar():
    return pl.BlockSpec(memory_space=pltpu.SMEM)


def ring_device(n, shift):
    here = lax.axis_index("ctx")
    place = jnp.where(lax.rem(here, 2) == 0, lax.div(here, 2), n - 1 - lax.div(here, 2))
    place = lax.rem(place + shift + n, n)
    return jnp.where(place < n // 2, 2 * place, 2 * (n - 1 - place) + 1)


def outside():
    return pl.BlockSpec(memory_space=pltpu.HBM)


def take(refs, parts, groups, rows):
    blocks, at = [], 0
    for count in parts:
        blocks.append(Block(refs[at : at + count], groups, rows))
        at += count
    return blocks, refs[at:]


def pack(token_mask, v):
    rows, width = v.shape
    groups = width // HEAD
    block = lax.axis_index("ctx")
    token = lax.broadcasted_iota(jnp.int32, (FLAG_ROWS, rows), 1)
    flags = ((token_mask[None, :] != 0) | ((block == 0) & (token == 0))).astype(BF16)
    v, flags = lax.optimization_barrier((v, flags))
    by_head = v.reshape(rows, groups, HEAD).transpose(1, 0, 2).reshape(groups * rows, HEAD)
    return jnp.concatenate([by_head, flags], 0)


def by_head_kernel(x_ref, o_ref):
    rows, width = x_ref.shape
    for g in range(width // HEAD):
        o_ref[g * rows : (g + 1) * rows, :] = x_ref[:, g * HEAD : (g + 1) * HEAD]


def by_head(x):
    return pl.pallas_call(
        by_head_kernel,
        out_shape=jax.ShapeDtypeStruct((x.size // HEAD, HEAD), BF16),
        in_specs=[whole()],
        out_specs=whole(),
        cost_estimate=pl.CostEstimate(flops=4 * 10**9, bytes_accessed=0, transcendentals=0),
        compiler_params=LIMIT,
        name="by_head",
    )(x)


def attend(blocks, g, q, biases):
    keys = jnp.concatenate([block.keys(g) for block in blocks], 0)
    scores = lax.dot_general(keys, q, NT, preferred_element_type=F32)
    results = []
    for i, (block, bias) in enumerate(zip(blocks, biases)):
        s = scores[i * block.rows : (i + 1) * block.rows] + bias
        m = jnp.max(s, axis=0, keepdims=True)
        p = jnp.exp2((s - m) * SCALE)
        l = jnp.sum(p, axis=0, keepdims=True)
        results.append((m, l, jnp.dot(block.values(g), p.astype(BF16), preferred_element_type=F32)))
    return results


def merge(parts):
    top = functools.reduce(jnp.maximum, [m for m, _, _ in parts])
    factors = [jnp.exp2((m - top) * SCALE) for m, _, _ in parts]
    total = sum(l * f for (_, l, _), f in zip(parts, factors))
    return top, total, sum(a * f for (_, _, a), f in zip(parts, factors))


def load_state(acc_ref, stat_ref, g, at):
    rows = slice(g * HEAD, (g + 1) * HEAD)
    return stat_ref[2 * g : 2 * g + 1, at], stat_ref[2 * g + 1 : 2 * g + 2, at], acc_ref[rows, at]


def store_state(acc_ref, stat_ref, g, at, state):
    stat_ref[2 * g : 2 * g + 1, at] = state[0]
    stat_ref[2 * g + 1 : 2 * g + 2, at] = state[1]
    acc_ref[g * HEAD : (g + 1) * HEAD, at] = state[2]


def first_kernel(groups, rows, live_ref, q_ref, k_ref, v_ref, stacked, acc, stat):
    n_q, width = q_ref.shape
    heads = width // HEAD // groups
    lanes = heads * n_q
    block = Block([k_ref, v_ref], groups, rows)
    bias = block.bias(lanes, lax.axis_index("ctx") < live_ref[0])
    for g in range(groups):
        q = jnp.concatenate(
            [q_ref[:, (g * heads + h) * HEAD : (g * heads + h + 1) * HEAD].astype(F32) for h in range(heads)], 0
        ).astype(BF16)
        stacked[g * lanes : (g + 1) * lanes, :] = q
        store_state(acc, stat, g, slice(None), attend([block], g, q, [bias])[0])


def state_shapes(groups, lanes):
    return [
        jax.ShapeDtypeStruct((groups * HEAD, lanes), F32),
        jax.ShapeDtypeStruct((2 * groups, lanes), F32),
    ]


def query_first(live_blocks, q, k, v, groups, rows):
    n_q, width = q.shape
    lanes = n_q * width // HEAD // groups
    return pl.pallas_call(
        functools.partial(first_kernel, groups, rows),
        out_shape=[jax.ShapeDtypeStruct((groups * lanes, HEAD), BF16)] + state_shapes(groups, lanes),
        in_specs=[scalar()] + [whole()] * 3,
        out_specs=[whole()] * 3,
        cost_estimate=pl.CostEstimate(flops=0, bytes_accessed=0, transcendentals=0),
        compiler_params=LIMIT,
        name="query_first",
    )(live_blocks, q, k, v)


def query_body(blocks, shifts, n, live_ref, groups, stacked, acc_in, stat_in, acc, stat):
    lanes = stacked.shape[0] // groups
    step = min(lanes, HEAD)
    biases = [block.bias(step, ring_device(n, shift) < live_ref[0]) for block, shift in zip(blocks, shifts)]
    for g in range(groups):
        for first in range(0, lanes, step):
            at = slice(first, first + step)
            q = stacked[g * lanes + first : g * lanes + first + step, :]
            parts = [load_state(acc_in, stat_in, g, at)] + attend(blocks, g, q, biases)
            store_state(acc, stat, g, at, merge(parts))


def more_kernel(groups, rows, parts, shifts, n, live_ref, stacked, acc_in, stat_in, *refs):
    blocks, (acc, stat) = take(refs, parts, groups, rows)
    query_body(blocks, shifts, n, live_ref, groups, stacked, acc_in, stat_in, acc, stat)


def query_more(live_blocks, stacked, acc, stat, pieces, shifts, n, groups, rows):
    operands = [part for piece in pieces for part in piece]
    return pl.pallas_call(
        functools.partial(more_kernel, groups, rows, [len(piece) for piece in pieces], shifts, n),
        out_shape=state_shapes(groups, stacked.shape[0] // groups),
        in_specs=[scalar()] + [whole()] * (3 + len(operands)),
        out_specs=[whole()] * 2,
        input_output_aliases={2: 0, 3: 1},
        compiler_params=LIMIT,
        name="query_more",
    )(live_blocks, stacked, acc, stat, *operands)


def context_body(groups, rows, live_ref, q_ref, anchor, own, o_ref, o_buf, out_sems):
    here = lax.axis_index("ctx")
    share = q_ref.shape[1] // groups
    spans = [pl.ds(g * share, share) for g in range(groups)]
    stores = [pltpu.make_async_copy(o_buf.at[:, at], o_ref.at[:, at], out_sems.at[g]) for g, at in enumerate(spans)]
    key = lax.broadcasted_iota(jnp.int32, (rows, rows), 0)
    row = lax.broadcasted_iota(jnp.int32, (rows, rows), 1)
    see_anchor = anchor.flags() * jnp.where(here > 0, 1.0, 0.0)
    see_own = jnp.where(key < row, own.flags(), jnp.where(key == row, 1.0, 0.0))
    bias = jnp.where(jnp.concatenate([see_anchor, see_own], 0) > 0.5, 0.0, HIDDEN)
    alive = jnp.where(here < live_ref[0], 1.0, 0.0)
    for g in range(groups):
        keys = jnp.concatenate([anchor.keys(g), own.keys(g)], 0)
        values = jnp.concatenate([anchor.values(g), own.values(g)], 1)
        for h in range(share // HEAD):
            at = slice(g * share + h * HEAD, g * share + (h + 1) * HEAD)
            s = lax.dot_general(keys, q_ref[:, at], NT, preferred_element_type=F32)
            s = s + bias
            m = jnp.max(s, axis=0, keepdims=True)
            p = jnp.exp2((s - m) * SCALE)
            l = jnp.sum(p, axis=0, keepdims=True)
            a = jnp.dot(values, p.astype(BF16), preferred_element_type=F32)
            o_buf[:, at] = jnp.transpose((a * (alive / l)).astype(BF16))
        stores[g].start()
    return stores


def both_kernel(groups, rows, devices, parts, shifts, n, aliased, live_ref, stacked, acc_in, stat_in, q_ref, own_k, own_v, *refs):
    blocks, rest = take(refs, parts, groups, rows)
    acc, stat, o_ref, anchor_k, anchor_v, o_buf, out_sems = rest[aliased:]
    here = lax.axis_index("ctx")
    for device, block in zip(devices, blocks):

        @pl.when(here == device)
        def _():
            anchor_k[...] = jnp.concatenate([block.keys(g) for g in range(groups)], 0)
            anchor_v[...] = block.v_ref[...]

    mine = functools.reduce(jnp.logical_or, [here == device for device in devices])
    first, own = Block([anchor_k, anchor_v], groups, rows), Block([own_k, own_v], groups, rows)

    @pl.when(mine)
    def _():
        stores = context_body(groups, rows, live_ref, q_ref, first, own, o_ref, o_buf, out_sems)
        query_body(blocks[-len(shifts) :], shifts, n, live_ref, groups, stacked, acc_in, stat_in, acc, stat)
        for store in stores:
            store.wait()

    @pl.when(jnp.logical_not(mine))
    def _():
        query_body(blocks[-len(shifts) :], shifts, n, live_ref, groups, stacked, acc_in, stat_in, acc, stat)


def both(live_blocks, stacked, acc, stat, q, own, anchors, shifts, n, groups, before=None):
    rows = own[0].shape[0]
    devices, pieces = zip(*anchors)
    parts = [len(piece) for piece in pieces]
    operands = [part for piece in pieces for part in piece]
    extra = [] if before is None else [before]
    return pl.pallas_call(
        functools.partial(both_kernel, groups, rows, devices, parts, shifts, n, len(extra)),
        out_shape=state_shapes(groups, stacked.shape[0] // groups) + [jax.ShapeDtypeStruct(q.shape, q.dtype)],
        in_specs=[scalar()] + [whole()] * (6 + len(operands)) + [outside()] * len(extra),
        out_specs=[whole()] * 2 + [outside()],
        input_output_aliases={2: 0, 3: 1} | ({7 + len(operands): 2} if extra else {}),
        scratch_shapes=[
            pltpu.VMEM((own[0].size // HEAD, HEAD), BF16),
            pltpu.VMEM(own[1].shape, BF16),
            pltpu.VMEM(q.shape, q.dtype),
            pltpu.SemaphoreType.DMA((groups,)),
        ],
        compiler_params=LIMIT,
        name="both",
    )(live_blocks, stacked, acc, stat, q, *own, *operands, *extra)


def finish_kernel(
    groups, rows, device, parts, n, live_ref, stacked, acc, stat, q_ref, own_k, own_v, *refs
):
    (block,), rest = take(refs, parts, groups, rows)
    _, query_ref, context_ref, buffer, out_sems, *buffers = rest
    lanes = stacked.shape[0] // groups
    n_q, width = buffer.shape
    heads = width // HEAD // groups
    share = heads * HEAD
    spans = [pl.ds(g * share, share) for g in range(groups)]
    stores = [
        pltpu.make_async_copy(buffer.at[:, at], query_ref.at[:, at], out_sems.at[g]) for g, at in enumerate(spans)
    ]
    bias = block.bias(lanes, ring_device(n, n // 2) < live_ref[0])
    for g in range(groups):
        q = stacked[g * lanes : (g + 1) * lanes, :]
        state = load_state(acc, stat, g, slice(None))
        _, total, part = merge([state] + attend([block], g, q, [bias]))
        out = part * (1.0 / total)
        out = jnp.transpose(out.astype(BF16)) if n_q % 16 == 0 else jnp.transpose(out)
        for h in range(heads):
            at = g * share + h * HEAD
            buffer[:, at : at + HEAD] = out[h * n_q : (h + 1) * n_q].astype(BF16)
        stores[g].start()

    @pl.when(lax.axis_index("ctx") == device)
    def _():
        own = Block([own_k, own_v], groups, rows)
        for store in context_body(groups, rows, live_ref, q_ref, block, own, context_ref, *buffers):
            store.wait()

    for store in stores:
        store.wait()


def finish(live_blocks, stacked, acc, stat, q, own, last, n, groups, shape, before):
    rows, width = q.shape
    device, piece = last
    return pl.pallas_call(
        functools.partial(finish_kernel, groups, rows, device, [len(piece)], n),
        out_shape=[shape, jax.ShapeDtypeStruct(q.shape, q.dtype)],
        in_specs=[scalar()] + [whole()] * (6 + len(piece)) + [outside()],
        out_specs=[outside()] * 2,
        input_output_aliases={7 + len(piece): 1},
        scratch_shapes=[
            pltpu.VMEM(shape.shape, shape.dtype),
            pltpu.SemaphoreType.DMA((groups,)),
            pltpu.VMEM(q.shape, q.dtype),
            pltpu.SemaphoreType.DMA((groups,)),
        ],
        compiler_params=LIMIT,
        name="finish",
    )(live_blocks, stacked, acc, stat, q, *own, *piece, before)


def local(context_q, context_k, context_v, question_q, token_mask, live_blocks):
    n = lax.axis_size("ctx")
    rows, width = context_k.shape
    groups = width // HEAD
    ring = list(range(0, n, 2)) + list(range(n - 1, 0, -2))
    forth = [(ring[i], ring[(i + 1) % n]) for i in range(n)]
    back = [(b, a) for a, b in forth]

    half = n // 2

    def send(value, pairs):
        return lax.ppermute(value, "ctx", pairs)

    packed = pack(token_mask, context_v)
    own = (context_k, packed)
    left_k = right_k = context_k
    left_v = right_v = packed
    state = context_output = None
    arrived, anchors = [], [(ring[0], own)]
    for step in range(1, half + 1):
        left_k, right_v = send(left_k, forth), send(right_v, back)
        if step < half:
            left_v, right_k = send(left_v, forth), send(right_k, back)
        pieces = [piece for _, piece in arrived]
        if step == 1:
            state = query_first(live_blocks, question_q, *own, groups, rows)
        elif step < half - 1:
            state = [state[0], *query_more(live_blocks, *state, pieces, (1 - step, step - 1), n, groups, rows)]
        else:
            new = anchors + arrived if step == half - 1 else arrived
            *update, context_output = both(
                live_blocks, *state, context_q, own, new, (1 - step, step - 1), n, groups, context_output
            )
            state = [state[0], *update]
        anchors += arrived
        if step < half:
            if step == 1:
                left_k = by_head(left_k)
                right_k = by_head(right_k)
            right_k, state = lax.optimization_barrier((right_k, state))
            arrived = [(ring[step], (left_k, left_v)), (ring[n - step], (right_k, right_v))]
    left, right = left_k, right_v
    query_output, context_output = finish(
        live_blocks,
        *state,
        context_q,
        own,
        (ring[half], (left, right)),
        n,
        groups,
        jax.ShapeDtypeStruct(question_q.shape, BF16),
        context_output,
    )
    return context_output, query_output


def solution(mesh):
    rows = P(("dp", "ctx"), None)
    return jax.shard_map(
        local,
        mesh=mesh,
        in_specs=(rows, rows, rows, rows, P(("dp", "ctx")), P("dp")),
        out_specs=(rows, rows),
        check_vma=False,
    )
```

```python
import functools
import math

import jax
import jax.numpy as jnp
from jax import lax
from jax.experimental import pallas as pl
from jax.experimental.pallas import tpu as pltpu
from jax.sharding import PartitionSpec as P

HEAD = 128
FLAG_ROWS = 16
HIDDEN = -1e30
SCALE = HEAD**-0.5 / math.log(2.0)
NT = (((1,), (1,)), ((), ()))
F32 = jnp.float32
BF16 = jnp.bfloat16
LIMIT = pltpu.CompilerParams(vmem_limit_bytes=24 * 1024 * 1024)


def whole():
    return pl.BlockSpec(memory_space=pltpu.VMEM)


class Block:
    def __init__(self, refs, groups, rows):
        self.groups, self.rows = groups, rows
        self.k_ref, self.v_ref = refs[0], refs[-1]
        self.v_base = groups * rows if len(refs) == 1 else 0

    def keys(self, g):
        if self.k_ref.shape[1] > HEAD:
            return self.k_ref[:, g * HEAD : (g + 1) * HEAD]
        return self.k_ref[g * self.rows : (g + 1) * self.rows, :]

    def values(self, g):
        at = self.v_base + g * self.rows
        return jnp.transpose(self.v_ref[at : at + self.rows, :])

    def flags(self):
        at = self.v_base + self.groups * self.rows
        flags = self.v_ref[at : at + FLAG_ROWS, :].astype(F32)[:1]
        return jnp.transpose(jnp.broadcast_to(flags, (self.rows, self.rows)))

    def bias(self, lanes, alive):
        flags = self.flags()
        while flags.shape[1] < lanes:
            flags = jnp.concatenate([flags, flags], 1)
        return jnp.where(flags[:, :lanes] > jnp.where(alive, 0.5, 2.0), 0.0, HIDDEN)


def scalar():
    return pl.BlockSpec(memory_space=pltpu.SMEM)


def ring_device(n, shift):
    here = lax.axis_index("ctx")
    place = jnp.where(lax.rem(here, 2) == 0, lax.div(here, 2), n - 1 - lax.div(here, 2))
    place = lax.rem(place + shift + n, n)
    return jnp.where(place < n // 2, 2 * place, 2 * (n - 1 - place) + 1)


def outside():
    return pl.BlockSpec(memory_space=pltpu.HBM)


def take(refs, parts, groups, rows):
    blocks, at = [], 0
    for count in parts:
        blocks.append(Block(refs[at : at + count], groups, rows))
        at += count
    return blocks, refs[at:]


def pack(token_mask, v):
    rows, width = v.shape
    groups = width // HEAD
    block = lax.axis_index("ctx")
    token = lax.broadcasted_iota(jnp.int32, (FLAG_ROWS, rows), 1)
    flags = ((token_mask[None, :] != 0) | ((block == 0) & (token == 0))).astype(BF16)
    v, flags = lax.optimization_barrier((v, flags))
    by_head = v.reshape(rows, groups, HEAD).transpose(1, 0, 2).reshape(groups * rows, HEAD)
    return jnp.concatenate([by_head, flags], 0)


def by_head_kernel(x_ref, o_ref):
    rows, width = x_ref.shape
    for g in range(width // HEAD):
        o_ref[g * rows : (g + 1) * rows, :] = x_ref[:, g * HEAD : (g + 1) * HEAD]


def by_head(x):
    return pl.pallas_call(
        by_head_kernel,
        out_shape=jax.ShapeDtypeStruct((x.size // HEAD, HEAD), BF16),
        in_specs=[whole()],
        out_specs=whole(),
        cost_estimate=pl.CostEstimate(flops=4 * 10**9, bytes_accessed=0, transcendentals=0),
        compiler_params=LIMIT,
        name="by_head",
    )(x)


def relay_kernel(x_ref, o_ref):
    o_ref[...] = x_ref[...]


def relay(x):
    return pl.pallas_call(
        relay_kernel,
        out_shape=jax.ShapeDtypeStruct(x.shape, x.dtype),
        in_specs=[whole()],
        out_specs=whole(),
        cost_estimate=pl.CostEstimate(flops=4 * 10**9, bytes_accessed=0, transcendentals=0),
        compiler_params=LIMIT,
        name="relay",
    )(x)


def attend(blocks, g, q, biases):
    keys = jnp.concatenate([block.keys(g) for block in blocks], 0)
    scores = lax.dot_general(keys, q, NT, preferred_element_type=F32)
    results = []
    for i, (block, bias) in enumerate(zip(blocks, biases)):
        s = scores[i * block.rows : (i + 1) * block.rows] + bias
        m = jnp.max(s, axis=0, keepdims=True)
        p = jnp.exp2((s - m) * SCALE)
        l = jnp.sum(p, axis=0, keepdims=True)
        results.append((m, l, jnp.dot(block.values(g), p.astype(BF16), preferred_element_type=F32)))
    return results


def merge(parts):
    top = functools.reduce(jnp.maximum, [m for m, _, _ in parts])
    factors = [jnp.exp2((m - top) * SCALE) for m, _, _ in parts]
    total = sum(l * f for (_, l, _), f in zip(parts, factors))
    return top, total, sum(a * f for (_, _, a), f in zip(parts, factors))


def load_state(acc_ref, stat_ref, g, at):
    rows = slice(g * HEAD, (g + 1) * HEAD)
    return stat_ref[2 * g : 2 * g + 1, at], stat_ref[2 * g + 1 : 2 * g + 2, at], acc_ref[rows, at]


def store_state(acc_ref, stat_ref, g, at, state):
    stat_ref[2 * g : 2 * g + 1, at] = state[0]
    stat_ref[2 * g + 1 : 2 * g + 2, at] = state[1]
    acc_ref[g * HEAD : (g + 1) * HEAD, at] = state[2]


def first_kernel(groups, rows, live_ref, q_ref, k_ref, v_ref, stacked, acc, stat):
    n_q, width = q_ref.shape
    heads = width // HEAD // groups
    lanes = heads * n_q
    block = Block([k_ref, v_ref], groups, rows)
    bias = block.bias(lanes, lax.axis_index("ctx") < live_ref[0])
    for g in range(groups):
        q = jnp.concatenate(
            [q_ref[:, (g * heads + h) * HEAD : (g * heads + h + 1) * HEAD].astype(F32) for h in range(heads)], 0
        ).astype(BF16)
        stacked[g * lanes : (g + 1) * lanes, :] = q
        store_state(acc, stat, g, slice(None), attend([block], g, q, [bias])[0])


def state_shapes(groups, lanes):
    return [
        jax.ShapeDtypeStruct((groups * HEAD, lanes), F32),
        jax.ShapeDtypeStruct((2 * groups, lanes), F32),
    ]


def query_first(live_blocks, q, k, v, groups, rows):
    n_q, width = q.shape
    lanes = n_q * width // HEAD // groups
    return pl.pallas_call(
        functools.partial(first_kernel, groups, rows),
        out_shape=[jax.ShapeDtypeStruct((groups * lanes, HEAD), BF16)] + state_shapes(groups, lanes),
        in_specs=[scalar()] + [whole()] * 3,
        out_specs=[whole()] * 3,
        cost_estimate=pl.CostEstimate(flops=0, bytes_accessed=0, transcendentals=0),
        compiler_params=LIMIT,
        name="query_first",
    )(live_blocks, q, k, v)


def query_body(blocks, shifts, n, live_ref, groups, stacked, acc_in, stat_in, acc, stat):
    lanes = stacked.shape[0] // groups
    step = min(lanes, HEAD)
    biases = [block.bias(step, ring_device(n, shift) < live_ref[0]) for block, shift in zip(blocks, shifts)]
    for g in range(groups):
        for first in range(0, lanes, step):
            at = slice(first, first + step)
            q = stacked[g * lanes + first : g * lanes + first + step, :]
            parts = [load_state(acc_in, stat_in, g, at)] + attend(blocks, g, q, biases)
            store_state(acc, stat, g, at, merge(parts))


def more_kernel(groups, rows, parts, shifts, n, live_ref, stacked, acc_in, stat_in, *refs):
    blocks, (acc, stat) = take(refs, parts, groups, rows)
    query_body(blocks, shifts, n, live_ref, groups, stacked, acc_in, stat_in, acc, stat)


def query_more(live_blocks, stacked, acc, stat, pieces, shifts, n, groups, rows):
    operands = [part for piece in pieces for part in piece]
    return pl.pallas_call(
        functools.partial(more_kernel, groups, rows, [len(piece) for piece in pieces], shifts, n),
        out_shape=state_shapes(groups, stacked.shape[0] // groups),
        in_specs=[scalar()] + [whole()] * (3 + len(operands)),
        out_specs=[whole()] * 2,
        input_output_aliases={2: 0, 3: 1},
        compiler_params=LIMIT,
        name="query_more",
    )(live_blocks, stacked, acc, stat, *operands)


def context_body(groups, rows, live_ref, q_ref, anchor, own, o_ref, o_buf, out_sems):
    here = lax.axis_index("ctx")
    share = q_ref.shape[1] // groups
    spans = [pl.ds(g * share, share) for g in range(groups)]
    stores = [pltpu.make_async_copy(o_buf.at[:, at], o_ref.at[:, at], out_sems.at[g]) for g, at in enumerate(spans)]
    key = lax.broadcasted_iota(jnp.int32, (rows, rows), 0)
    row = lax.broadcasted_iota(jnp.int32, (rows, rows), 1)
    see_anchor = anchor.flags() * jnp.where(here > 0, 1.0, 0.0)
    see_own = jnp.where(key < row, own.flags(), jnp.where(key == row, 1.0, 0.0))
    bias = jnp.where(jnp.concatenate([see_anchor, see_own], 0) > 0.5, 0.0, HIDDEN)
    alive = jnp.where(here < live_ref[0], 1.0, 0.0)
    all_keys = [jnp.concatenate([anchor.keys(g), own.keys(g)], 0) for g in range(groups)]
    all_values = [jnp.concatenate([anchor.values(g), own.values(g)], 1) for g in range(groups)]
    for g in range(groups):
        keys = all_keys[g]
        values = all_values[g]
        for h in range(share // HEAD):
            at = slice(g * share + h * HEAD, g * share + (h + 1) * HEAD)
            s = lax.dot_general(keys, q_ref[:, at], NT, preferred_element_type=F32)
            s = s + bias
            m = jnp.max(s, axis=0, keepdims=True)
            p = jnp.exp2((s - m) * SCALE)
            l = jnp.sum(p, axis=0, keepdims=True)
            a = jnp.dot(values, p.astype(BF16), preferred_element_type=F32)
            o_buf[:, at] = jnp.transpose((a * (alive / l)).astype(BF16))
        stores[g].start()
    return stores


def both_kernel(groups, rows, devices, parts, shifts, n, aliased, live_ref, stacked, acc_in, stat_in, q_ref, own_k, own_v, *refs):
    blocks, rest = take(refs, parts, groups, rows)
    acc, stat, o_ref, anchor_k, anchor_v, o_buf, out_sems = rest[aliased:]
    here = lax.axis_index("ctx")
    for device, block in zip(devices, blocks):

        @pl.when(here == device)
        def _():
            anchor_k[...] = jnp.concatenate([block.keys(g) for g in range(groups)], 0)
            anchor_v[...] = block.v_ref[...]

    mine = functools.reduce(jnp.logical_or, [here == device for device in devices])
    first, own = Block([anchor_k, anchor_v], groups, rows), Block([own_k, own_v], groups, rows)

    @pl.when(mine)
    def _():
        stores = context_body(groups, rows, live_ref, q_ref, first, own, o_ref, o_buf, out_sems)
        query_body(blocks[-len(shifts) :], shifts, n, live_ref, groups, stacked, acc_in, stat_in, acc, stat)
        for store in stores:
            store.wait()

    @pl.when(jnp.logical_not(mine))
    def _():
        query_body(blocks[-len(shifts) :], shifts, n, live_ref, groups, stacked, acc_in, stat_in, acc, stat)


def both(live_blocks, stacked, acc, stat, q, own, anchors, shifts, n, groups, before=None):
    rows = own[0].shape[0]
    devices, pieces = zip(*anchors)
    parts = [len(piece) for piece in pieces]
    operands = [part for piece in pieces for part in piece]
    extra = [] if before is None else [before]
    return pl.pallas_call(
        functools.partial(both_kernel, groups, rows, devices, parts, shifts, n, len(extra)),
        out_shape=state_shapes(groups, stacked.shape[0] // groups) + [jax.ShapeDtypeStruct(q.shape, q.dtype)],
        in_specs=[scalar()] + [whole()] * (6 + len(operands)) + [outside()] * len(extra),
        out_specs=[whole()] * 2 + [outside()],
        input_output_aliases={2: 0, 3: 1} | ({7 + len(operands): 2} if extra else {}),
        scratch_shapes=[
            pltpu.VMEM((own[0].size // HEAD, HEAD), BF16),
            pltpu.VMEM(own[1].shape, BF16),
            pltpu.VMEM(q.shape, q.dtype),
            pltpu.SemaphoreType.DMA((groups,)),
        ],
        compiler_params=LIMIT,
        name="both",
    )(live_blocks, stacked, acc, stat, q, *own, *operands, *extra)


def finish_kernel(
    groups, rows, device, parts, n, live_ref, stacked, acc, stat, q_ref, own_k, own_v, *refs
):
    (block,), rest = take(refs, parts, groups, rows)
    _, query_ref, context_ref, buffer, out_sems, *buffers = rest
    lanes = stacked.shape[0] // groups
    n_q, width = buffer.shape
    heads = width // HEAD // groups
    share = heads * HEAD
    spans = [pl.ds(g * share, share) for g in range(groups)]
    stores = [
        pltpu.make_async_copy(buffer.at[:, at], query_ref.at[:, at], out_sems.at[g]) for g, at in enumerate(spans)
    ]
    bias = block.bias(lanes, ring_device(n, n // 2) < live_ref[0])
    for g in range(groups):
        q = stacked[g * lanes : (g + 1) * lanes, :]
        state = load_state(acc, stat, g, slice(None))
        _, total, part = merge([state] + attend([block], g, q, [bias]))
        out = part * (1.0 / total)
        out = jnp.transpose(out.astype(BF16)) if n_q % 16 == 0 else jnp.transpose(out)
        for h in range(heads):
            at = g * share + h * HEAD
            buffer[:, at : at + HEAD] = out[h * n_q : (h + 1) * n_q].astype(BF16)
        stores[g].start()

    @pl.when(lax.axis_index("ctx") == device)
    def _():
        own = Block([own_k, own_v], groups, rows)
        for store in context_body(groups, rows, live_ref, q_ref, block, own, context_ref, *buffers):
            store.wait()

    for store in stores:
        store.wait()


def finish(live_blocks, stacked, acc, stat, q, own, last, n, groups, shape, before):
    rows, width = q.shape
    device, piece = last
    return pl.pallas_call(
        functools.partial(finish_kernel, groups, rows, device, [len(piece)], n),
        out_shape=[shape, jax.ShapeDtypeStruct(q.shape, q.dtype)],
        in_specs=[scalar()] + [whole()] * (6 + len(piece)) + [outside()],
        out_specs=[outside()] * 2,
        input_output_aliases={7 + len(piece): 1},
        scratch_shapes=[
            pltpu.VMEM(shape.shape, shape.dtype),
            pltpu.SemaphoreType.DMA((groups,)),
            pltpu.VMEM(q.shape, q.dtype),
            pltpu.SemaphoreType.DMA((groups,)),
        ],
        compiler_params=LIMIT,
        name="finish",
    )(live_blocks, stacked, acc, stat, q, *own, *piece, before)


def local(context_q, context_k, context_v, question_q, token_mask, live_blocks):
    n = lax.axis_size("ctx")
    rows, width = context_k.shape
    groups = width // HEAD
    ring = list(range(0, n, 2)) + list(range(n - 1, 0, -2))
    forth = [(ring[i], ring[(i + 1) % n]) for i in range(n)]
    back = [(b, a) for a, b in forth]

    half = n // 2

    def send(value, pairs):
        return lax.ppermute(value, "ctx", pairs)

    packed = pack(token_mask, context_v)
    own = (context_k, packed)
    left_k = right_k = context_k
    left_v = right_v = packed
    state = context_output = None
    arrived, anchors = [], [(ring[0], own)]
    for step in range(1, half + 1):
        left_k, right_v = send(left_k, forth), send(right_v, back)
        if step < half:
            left_v, right_k = send(left_v, forth), send(right_k, back)
        pieces = [piece for _, piece in arrived]
        if step == 1:
            state = query_first(live_blocks, question_q, *own, groups, rows)
        elif step < half - 1:
            state = [state[0], *query_more(live_blocks, *state, pieces, (1 - step, step - 1), n, groups, rows)]
        else:
            new = anchors + arrived if step == half - 1 else arrived
            *update, context_output = both(
                live_blocks, *state, context_q, own, new, (1 - step, step - 1), n, groups, context_output
            )
            state = [state[0], *update]
        anchors += arrived
        if step < half:
            if step == 1:
                left_k = by_head(left_k)
                right_k = by_head(right_k)
            if step == 2:
                right_k = relay(right_k)
            right_k, state = lax.optimization_barrier((right_k, state))
            arrived = [(ring[step], (left_k, left_v)), (ring[n - step], (right_k, right_v))]
    left, right = left_k, right_v
    query_output, context_output = finish(
        live_blocks,
        *state,
        context_q,
        own,
        (ring[half], (left, right)),
        n,
        groups,
        jax.ShapeDtypeStruct(question_q.shape, BF16),
        context_output,
    )
    return context_output, query_output


def solution(mesh):
    rows = P(("dp", "ctx"), None)
    return jax.shard_map(
        local,
        mesh=mesh,
        in_specs=(rows, rows, rows, rows, P(("dp", "ctx")), P("dp")),
        out_specs=(rows, rows),
        check_vma=False,
    )
```

```python
import functools
import math

import jax
import jax.numpy as jnp
from jax import lax
from jax.experimental import pallas as pl
from jax.experimental.pallas import tpu as pltpu
from jax.sharding import PartitionSpec as P

HEAD = 128
FLAG_ROWS = 16
HIDDEN = -1e30
SCALE = HEAD**-0.5 / math.log(2.0)
NT = (((1,), (1,)), ((), ()))
F32 = jnp.float32
BF16 = jnp.bfloat16
LIMIT = pltpu.CompilerParams(vmem_limit_bytes=24 * 1024 * 1024)


def whole():
    return pl.BlockSpec(memory_space=pltpu.VMEM)


class Block:
    def __init__(self, refs, groups, rows):
        self.groups, self.rows = groups, rows
        self.k_ref, self.v_ref = refs[0], refs[-1]
        self.v_base = groups * rows if len(refs) == 1 else 0

    def keys(self, g):
        if self.k_ref.shape[1] > HEAD:
            return self.k_ref[:, g * HEAD : (g + 1) * HEAD]
        return self.k_ref[g * self.rows : (g + 1) * self.rows, :]

    def values(self, g):
        at = self.v_base + g * self.rows
        return jnp.transpose(self.v_ref[at : at + self.rows, :])

    def flags(self):
        at = self.v_base + self.groups * self.rows
        flags = self.v_ref[at : at + FLAG_ROWS, :].astype(F32)[:1]
        return jnp.transpose(jnp.broadcast_to(flags, (self.rows, self.rows)))

    def bias(self, lanes, alive):
        flags = self.flags()
        while flags.shape[1] < lanes:
            flags = jnp.concatenate([flags, flags], 1)
        return jnp.where(flags[:, :lanes] > jnp.where(alive, 0.5, 2.0), 0.0, HIDDEN)


def scalar():
    return pl.BlockSpec(memory_space=pltpu.SMEM)


def ring_device(n, shift):
    here = lax.axis_index("ctx")
    place = jnp.where(lax.rem(here, 2) == 0, lax.div(here, 2), n - 1 - lax.div(here, 2))
    place = lax.rem(place + shift + n, n)
    return jnp.where(place < n // 2, 2 * place, 2 * (n - 1 - place) + 1)


def outside():
    return pl.BlockSpec(memory_space=pltpu.HBM)


def take(refs, parts, groups, rows):
    blocks, at = [], 0
    for count in parts:
        blocks.append(Block(refs[at : at + count], groups, rows))
        at += count
    return blocks, refs[at:]


def pack(token_mask, v):
    rows, width = v.shape
    groups = width // HEAD
    block = lax.axis_index("ctx")
    token = lax.broadcasted_iota(jnp.int32, (FLAG_ROWS, rows), 1)
    flags = ((token_mask[None, :] != 0) | ((block == 0) & (token == 0))).astype(BF16)
    v, flags = lax.optimization_barrier((v, flags))
    by_head = v.reshape(rows, groups, HEAD).transpose(1, 0, 2).reshape(groups * rows, HEAD)
    return jnp.concatenate([by_head, flags], 0)


def by_head_kernel(x_ref, o_ref):
    rows, width = x_ref.shape
    for g in range(width // HEAD):
        o_ref[g * rows : (g + 1) * rows, :] = x_ref[:, g * HEAD : (g + 1) * HEAD]


def by_head(x):
    return pl.pallas_call(
        by_head_kernel,
        out_shape=jax.ShapeDtypeStruct((x.size // HEAD, HEAD), BF16),
        in_specs=[whole()],
        out_specs=whole(),
        cost_estimate=pl.CostEstimate(flops=4 * 10**9, bytes_accessed=0, transcendentals=0),
        compiler_params=LIMIT,
        name="by_head",
    )(x)


def attend(blocks, g, q, biases):
    keys = jnp.concatenate([block.keys(g) for block in blocks], 0)
    scores = lax.dot_general(keys, q, NT, preferred_element_type=F32)
    results = []
    for i, (block, bias) in enumerate(zip(blocks, biases)):
        s = scores[i * block.rows : (i + 1) * block.rows] + bias
        m = jnp.max(s, axis=0, keepdims=True)
        p = jnp.exp2((s - m) * SCALE)
        l = jnp.sum(p, axis=0, keepdims=True)
        results.append((m, l, jnp.dot(block.values(g), p.astype(BF16), preferred_element_type=F32)))
    return results


def merge(parts):
    top = functools.reduce(jnp.maximum, [m for m, _, _ in parts])
    factors = [jnp.exp2((m - top) * SCALE) for m, _, _ in parts]
    total = sum(l * f for (_, l, _), f in zip(parts, factors))
    return top, total, sum(a * f for (_, _, a), f in zip(parts, factors))


def load_state(acc_ref, stat_ref, g, at):
    rows = slice(g * HEAD, (g + 1) * HEAD)
    return stat_ref[2 * g : 2 * g + 1, at], stat_ref[2 * g + 1 : 2 * g + 2, at], acc_ref[rows, at]


def store_state(acc_ref, stat_ref, g, at, state):
    stat_ref[2 * g : 2 * g + 1, at] = state[0]
    stat_ref[2 * g + 1 : 2 * g + 2, at] = state[1]
    acc_ref[g * HEAD : (g + 1) * HEAD, at] = state[2]


def first_kernel(groups, rows, live_ref, q_ref, k_ref, v_ref, stacked, acc, stat):
    n_q, width = q_ref.shape
    heads = width // HEAD // groups
    lanes = heads * n_q
    block = Block([k_ref, v_ref], groups, rows)
    bias = block.bias(lanes, lax.axis_index("ctx") < live_ref[0])
    for g in range(groups):
        q = jnp.concatenate(
            [q_ref[:, (g * heads + h) * HEAD : (g * heads + h + 1) * HEAD].astype(F32) for h in range(heads)], 0
        ).astype(BF16)
        stacked[g * lanes : (g + 1) * lanes, :] = q
        store_state(acc, stat, g, slice(None), attend([block], g, q, [bias])[0])


def state_shapes(groups, lanes):
    return [
        jax.ShapeDtypeStruct((groups * HEAD, lanes), F32),
        jax.ShapeDtypeStruct((2 * groups, lanes), F32),
    ]


def query_first(live_blocks, q, k, v, groups, rows):
    n_q, width = q.shape
    lanes = n_q * width // HEAD // groups
    return pl.pallas_call(
        functools.partial(first_kernel, groups, rows),
        out_shape=[jax.ShapeDtypeStruct((groups * lanes, HEAD), BF16)] + state_shapes(groups, lanes),
        in_specs=[scalar()] + [whole()] * 3,
        out_specs=[whole()] * 3,
        cost_estimate=pl.CostEstimate(flops=0, bytes_accessed=0, transcendentals=0),
        compiler_params=LIMIT,
        name="query_first",
    )(live_blocks, q, k, v)


def query_body(blocks, shifts, n, live_ref, groups, stacked, acc_in, stat_in, acc, stat):
    lanes = stacked.shape[0] // groups
    step = min(lanes, HEAD)
    biases = [block.bias(step, ring_device(n, shift) < live_ref[0]) for block, shift in zip(blocks, shifts)]
    for g in range(groups):
        for first in range(0, lanes, step):
            at = slice(first, first + step)
            q = stacked[g * lanes + first : g * lanes + first + step, :]
            parts = [load_state(acc_in, stat_in, g, at)] + attend(blocks, g, q, biases)
            store_state(acc, stat, g, at, merge(parts))


def more_kernel(groups, rows, parts, shifts, n, live_ref, stacked, acc_in, stat_in, *refs):
    blocks, (acc, stat) = take(refs, parts, groups, rows)
    query_body(blocks, shifts, n, live_ref, groups, stacked, acc_in, stat_in, acc, stat)


def query_more(live_blocks, stacked, acc, stat, pieces, shifts, n, groups, rows):
    operands = [part for piece in pieces for part in piece]
    return pl.pallas_call(
        functools.partial(more_kernel, groups, rows, [len(piece) for piece in pieces], shifts, n),
        out_shape=state_shapes(groups, stacked.shape[0] // groups),
        in_specs=[scalar()] + [whole()] * (3 + len(operands)),
        out_specs=[whole()] * 2,
        input_output_aliases={2: 0, 3: 1},
        compiler_params=LIMIT,
        name="query_more",
    )(live_blocks, stacked, acc, stat, *operands)


def context_body(groups, rows, live_ref, q_ref, anchor, own, o_ref, o_buf, out_sems):
    here = lax.axis_index("ctx")
    share = q_ref.shape[1] // groups
    spans = [pl.ds(g * share, share) for g in range(groups)]
    stores = [pltpu.make_async_copy(o_buf.at[:, at], o_ref.at[:, at], out_sems.at[g]) for g, at in enumerate(spans)]
    key = lax.broadcasted_iota(jnp.int32, (rows, rows), 0)
    row = lax.broadcasted_iota(jnp.int32, (rows, rows), 1)
    see_anchor = anchor.flags() * jnp.where(here > 0, 1.0, 0.0)
    see_own = jnp.where(key < row, own.flags(), jnp.where(key == row, 1.0, 0.0))
    bias = jnp.where(jnp.concatenate([see_anchor, see_own], 0) > 0.5, 0.0, HIDDEN)
    alive = jnp.where(here < live_ref[0], 1.0, 0.0)
    all_keys = [jnp.concatenate([anchor.keys(g), own.keys(g)], 0) for g in range(groups)]
    all_values = [jnp.concatenate([anchor.values(g), own.values(g)], 1) for g in range(groups)]
    for g in range(groups):
        keys = all_keys[g]
        values = all_values[g]
        for h in range(share // HEAD):
            at = slice(g * share + h * HEAD, g * share + (h + 1) * HEAD)
            s = lax.dot_general(keys, q_ref[:, at], NT, preferred_element_type=F32)
            s = s + bias
            m = jnp.max(s, axis=0, keepdims=True)
            p = jnp.exp2((s - m) * SCALE)
            l = jnp.sum(p, axis=0, keepdims=True)
            a = jnp.dot(values, p.astype(BF16), preferred_element_type=F32)
            o_buf[:, at] = jnp.transpose((a * (alive / l)).astype(BF16))
        stores[g].start()
    return stores


def both_kernel(groups, rows, devices, parts, shifts, n, aliased, live_ref, stacked, acc_in, stat_in, q_ref, own_k, own_v, *refs):
    blocks, rest = take(refs, parts, groups, rows)
    acc, stat, o_ref, anchor_k, anchor_v, o_buf, out_sems = rest[aliased:]
    here = lax.axis_index("ctx")
    own = Block([own_k, own_v], groups, rows)
    mine = functools.reduce(jnp.logical_or, [here == device for device in devices])

    def answer(first):
        stores = context_body(groups, rows, live_ref, q_ref, first, own, o_ref, o_buf, out_sems)
        query_body(blocks[-len(shifts) :], shifts, n, live_ref, groups, stacked, acc_in, stat_in, acc, stat)
        for store in stores:
            store.wait()

    if len(blocks) == len(shifts):
        for device, block in zip(devices, blocks):
            pl.when(here == device)(functools.partial(answer, block))
    else:
        for device, block in zip(devices, blocks):

            @pl.when(here == device)
            def _():
                anchor_k[...] = jnp.concatenate([block.keys(g) for g in range(groups)], 0)
                anchor_v[...] = block.v_ref[...]

        pl.when(mine)(functools.partial(answer, Block([anchor_k, anchor_v], groups, rows)))

    @pl.when(jnp.logical_not(mine))
    def _():
        query_body(blocks[-len(shifts) :], shifts, n, live_ref, groups, stacked, acc_in, stat_in, acc, stat)


def both(live_blocks, stacked, acc, stat, q, own, anchors, shifts, n, groups, before=None):
    rows = own[0].shape[0]
    devices, pieces = zip(*anchors)
    parts = [len(piece) for piece in pieces]
    operands = [part for piece in pieces for part in piece]
    extra = [] if before is None else [before]
    return pl.pallas_call(
        functools.partial(both_kernel, groups, rows, devices, parts, shifts, n, len(extra)),
        out_shape=state_shapes(groups, stacked.shape[0] // groups) + [jax.ShapeDtypeStruct(q.shape, q.dtype)],
        in_specs=[scalar()] + [whole()] * (6 + len(operands)) + [outside()] * len(extra),
        out_specs=[whole()] * 2 + [outside()],
        input_output_aliases={2: 0, 3: 1} | ({7 + len(operands): 2} if extra else {}),
        scratch_shapes=[
            pltpu.VMEM((own[0].size // HEAD, HEAD), BF16),
            pltpu.VMEM(own[1].shape, BF16),
            pltpu.VMEM(q.shape, q.dtype),
            pltpu.SemaphoreType.DMA((groups,)),
        ],
        compiler_params=LIMIT,
        name="both",
    )(live_blocks, stacked, acc, stat, q, *own, *operands, *extra)


def finish_kernel(
    groups, rows, device, parts, n, live_ref, stacked, acc, stat, q_ref, own_k, own_v, *refs
):
    (block,), rest = take(refs, parts, groups, rows)
    _, query_ref, context_ref, buffer, out_sems, *buffers = rest
    lanes = stacked.shape[0] // groups
    n_q, width = buffer.shape
    heads = width // HEAD // groups
    share = heads * HEAD
    spans = [pl.ds(g * share, share) for g in range(groups)]
    stores = [
        pltpu.make_async_copy(buffer.at[:, at], query_ref.at[:, at], out_sems.at[g]) for g, at in enumerate(spans)
    ]
    bias = block.bias(lanes, ring_device(n, n // 2) < live_ref[0])
    for g in range(groups):
        q = stacked[g * lanes : (g + 1) * lanes, :]
        state = load_state(acc, stat, g, slice(None))
        _, total, part = merge([state] + attend([block], g, q, [bias]))
        out = part * (1.0 / total)
        out = jnp.transpose(out.astype(BF16)) if n_q % 16 == 0 else jnp.transpose(out)
        for h in range(heads):
            at = g * share + h * HEAD
            buffer[:, at : at + HEAD] = out[h * n_q : (h + 1) * n_q].astype(BF16)
        stores[g].start()

    @pl.when(lax.axis_index("ctx") == device)
    def _():
        own = Block([own_k, own_v], groups, rows)
        for store in context_body(groups, rows, live_ref, q_ref, block, own, context_ref, *buffers):
            store.wait()

    for store in stores:
        store.wait()


def finish(live_blocks, stacked, acc, stat, q, own, last, n, groups, shape, before):
    rows, width = q.shape
    device, piece = last
    return pl.pallas_call(
        functools.partial(finish_kernel, groups, rows, device, [len(piece)], n),
        out_shape=[shape, jax.ShapeDtypeStruct(q.shape, q.dtype)],
        in_specs=[scalar()] + [whole()] * (6 + len(piece)) + [outside()],
        out_specs=[outside()] * 2,
        input_output_aliases={7 + len(piece): 1},
        scratch_shapes=[
            pltpu.VMEM(shape.shape, shape.dtype),
            pltpu.SemaphoreType.DMA((groups,)),
            pltpu.VMEM(q.shape, q.dtype),
            pltpu.SemaphoreType.DMA((groups,)),
        ],
        compiler_params=LIMIT,
        name="finish",
    )(live_blocks, stacked, acc, stat, q, *own, *piece, before)


def local(context_q, context_k, context_v, question_q, token_mask, live_blocks):
    n = lax.axis_size("ctx")
    rows, width = context_k.shape
    groups = width // HEAD
    ring = list(range(0, n, 2)) + list(range(n - 1, 0, -2))
    forth = [(ring[i], ring[(i + 1) % n]) for i in range(n)]
    back = [(b, a) for a, b in forth]

    half = n // 2

    def send(value, pairs):
        return lax.ppermute(value, "ctx", pairs)

    packed = pack(token_mask, context_v)
    own = (context_k, packed)
    left_k = right_k = context_k
    left_v = right_v = packed
    state = context_output = None
    arrived, anchors = [], [(ring[0], own)]
    for step in range(1, half + 1):
        left_k, right_v = send(left_k, forth), send(right_v, back)
        if step < half:
            left_v, right_k = send(left_v, forth), send(right_k, back)
        pieces = [piece for _, piece in arrived]
        if step == 1:
            state = query_first(live_blocks, question_q, *own, groups, rows)
        elif step < half - 1:
            state = [state[0], *query_more(live_blocks, *state, pieces, (1 - step, step - 1), n, groups, rows)]
        else:
            new = anchors + arrived if step == half - 1 else arrived
            *update, context_output = both(
                live_blocks, *state, context_q, own, new, (1 - step, step - 1), n, groups, context_output
            )
            state = [state[0], *update]
        anchors += arrived
        if step < half:
            if step == 1:
                left_k = by_head(left_k)
                right_k = by_head(right_k)
            right_k, state = lax.optimization_barrier((right_k, state))
            arrived = [(ring[step], (left_k, left_v)), (ring[n - step], (right_k, right_v))]
    left, right = left_k, right_v
    query_output, context_output = finish(
        live_blocks,
        *state,
        context_q,
        own,
        (ring[half], (left, right)),
        n,
        groups,
        jax.ShapeDtypeStruct(question_q.shape, BF16),
        context_output,
    )
    return context_output, query_output


def solution(mesh):
    rows = P(("dp", "ctx"), None)
    return jax.shard_map(
        local,
        mesh=mesh,
        in_specs=(rows, rows, rows, rows, P(("dp", "ctx")), P("dp")),
        out_specs=(rows, rows),
        check_vma=False,
    )
```
